32 devices in a mesh: space: 16 (over z, y, x), tm: 2 (over core).
Axes of the slice: x: 2, y: 2, z: 4, core: 2. Of those that a mesh axis runs over, the one named last changes fastest.
Arguments:
- snapshots: bfloat16 [262144, 512], P(('space', 'tm')), may hold values from -6 to 6
- range_test: bfloat16 [512, 128], replicated, may hold values from -0.25 to 0.25
- test_rows: bfloat16 [256, 262144], P(None, ('space', 'tm')), may hold values from -0.01171875 to 0.01171875
- species: int32 [256, 1024], P(('space', 'tm')), may hold values from 0 to 3
- reaction_rates: float32 [4], replicated, may hold values from 1 to 8
- adjoint_end: float32 [256, 1024], P(('space', 'tm')), may hold values from -6 to 6
Outputs:
- adjoint: float32 [256, 1024], P(('space', 'tm'))
- time_factors: float32 [128, 512], P(None, ('space', 'tm'))
The draws below stay inside these ranges and needn't reach their ends.
All inputs are finite; a program needn't handle non-finite values.
Results may differ from the reference program's by a relative error of at most 0.0012.
Values sent between devices are 32-bit elements; how exact they have to be, the bound alone decides.
No kernel may reach another device: no remote copies, remote signals or barrier semaphores. Data moves between devices by JAX's collectives and lax.ppermute only.
A program may use at most 64 MiB of HBM per device.

```python
import math
import jax
import jax.numpy as jnp
from jax import lax

GY = 1024
TIMES = 512
RANK = 128
SKETCH = 256
SPECIES = 4
NX = 256
CELLS = 262144


def set_ends(entries, key, smallest, high):
    extent = entries.shape
    index_at = [jax.random.randint(jax.random.fold_in(key, axis), (), 0, extent[axis]) for axis in range(len(extent))]
    entries = entries.at[tuple(index_at)].set(smallest)
    longest = extent.index(max(extent))
    index_at[longest] = (index_at[longest] + 1) % extent[longest]
    return entries.at[tuple(index_at)].set(high)


def block_levels(key, extent, pieces, low, largest):
    gain = 1.0
    for position, blocks in pieces:
        heights = jax.random.uniform(jax.random.fold_in(jax.random.fold_in(key, 6), position), (blocks,), jnp.float32, low / len(pieces), largest / len(pieces))
        gain = gain * jnp.repeat(jnp.exp(heights), extent[position] // blocks).reshape((-1,) + (1,) * (len(extent) - 1 - position))
    return gain


def normal_values(own_key, shape, width, bound, pieces=(), held_as=jnp.bfloat16):
    drawn = jax.random.normal(own_key, shape, jnp.float32) * width
    if len(pieces) > 0:
        drawn = block_levels(own_key, shape, pieces, -0.22, 0.18) * drawn
    return jnp.clip(drawn, min=-bound, max=bound).astype(held_as)


def setup_inputs(seed: int = 0) -> dict:
    splits = jax.random.split(jax.random.key(seed), 7)
    return {
        "snapshots": normal_values(splits[0], (CELLS, TIMES), 1.0, 6.0, ((0, 32),)),
        "range_test": normal_values(splits[1], (TIMES, RANK), TIMES ** -0.5, 0.25),
        "test_rows": normal_values(splits[2], (SKETCH, CELLS), CELLS ** -0.5, 0.01171875, ((1, 32),)),
        "species": set_ends(jax.random.randint(splits[3], (NX, GY), 0, SPECIES), jax.random.fold_in(splits[3], 1), 0, SPECIES - 1).astype(jnp.int32),
        "reaction_rates": jnp.clip(jnp.exp(jax.random.uniform(splits[4], (SPECIES,), jnp.float32, math.log(1.0), math.log(8.0))), 1.0, 8.0),
        "adjoint_end": normal_values(splits[5], (NX, GY), 1.0, 6.0, ((0, 32),), jnp.float32),
    }


DIFFUSION = 0.2
STEP_SIZE = 0.05

def laplace(field):
    padded = jnp.pad(field, 1)
    return padded[2:, 1:-1] + padded[:-2, 1:-1] + padded[1:-1, 2:] + padded[1:-1, :-2] - 4.0 * field

def reference(snapshots, range_test, test_rows, species, reaction_rates, adjoint_end):
    high = lax.Precision.HIGHEST
    range_part = jnp.dot(snapshots.astype(jnp.float32), range_test.astype(jnp.float32), preferred_element_type=jnp.float32)
    gram = jnp.dot(range_part.T, range_part, precision=high)
    lower_factor = jnp.linalg.cholesky(gram)
    basis = jax.scipy.linalg.solve_triangular(lower_factor, range_part.T, lower=True).T
    projected = jnp.dot(test_rows.astype(jnp.float32), basis, precision=high)
    corange = jnp.dot(test_rows.astype(jnp.float32), snapshots.astype(jnp.float32), preferred_element_type=jnp.float32)
    normal_matrix = jnp.dot(projected.T, projected, precision=high)
    normal_factor = jnp.linalg.cholesky(normal_matrix)
    moments = jnp.dot(projected.T, corange, precision=high)
    factors = jax.scipy.linalg.cho_solve((normal_factor, True), moments)
    states = jnp.dot(basis, factors[:, TIMES - 2:], precision=high)
    coupling = reaction_rates[species]
    adjoint = adjoint_end
    for column in (1, 0):
        state = states[:, column].reshape(NX, GY)
        adjoint = adjoint + DIFFUSION * laplace(adjoint) + STEP_SIZE * coupling * (1.0 - 3.0 * state * state) * adjoint
    return (adjoint, factors * CELLS ** (-0.5))
```

```python
import functools

import jax
import jax.numpy as jnp
from jax import lax
from jax.experimental import pallas as pl
from jax.experimental.pallas import tpu as pltpu
from jax.sharding import PartitionSpec as P

DIFFUSION = 0.2
STEP_SIZE = 0.05
AXES = ("space", "tm")
HIGH = lax.Precision.HIGHEST
NT = (((1,), (1,)), ((), ()))
F32 = jnp.float32
BF16 = jnp.bfloat16


def sketch_kernel(snap, test, om, range_t, ct, crit, om_t, corange, gram):
    step = pl.program_id(0)
    rank = om.shape[1]
    sketch = test.shape[0]
    times = snap.shape[1]

    @pl.when(step == 0)
    def _():
        om_t[...] = om[...].astype(F32).T.astype(BF16)
        corange[...] = jnp.zeros_like(corange)
        gram[...] = jnp.zeros_like(gram)

    states = snap[...]
    rt = lax.dot_general(om_t[...], states, NT, preferred_element_type=F32)
    range_t[...] = rt
    upper = rt.astype(BF16)
    lower = (rt - upper.astype(F32)).astype(BF16)
    both = jnp.concatenate([upper, lower], axis=0)
    gram[...] += lax.dot_general(both, both, NT, preferred_element_type=F32)
    corange[...] += jnp.dot(test[...], states, preferred_element_type=F32)

    @pl.when(step == pl.num_programs(0) - 1)
    def _():
        whole = corange[...]
        projected = jnp.dot(whole, om[...].astype(F32), precision=HIGH, preferred_element_type=F32)
        crit[0:sketch, :] = projected
        cross = gram[0:rank, rank:]
        crit[sketch:, :] = gram[0:rank, 0:rank] + cross + cross.T
        half = sketch // 2
        for h in range(2):
            turned = whole[h * half : (h + 1) * half, :].T
            ct[h] = turned
            for j in range(2):
                row = turned[times - 2 + j : times - 1 + j, :]
                for q in range(2):
                    place = sketch + j * 4 + h * 2 + q
                    crit[place : place + 1, rank // 2 :] = row[:, q * 64 : (q + 1) * 64]


def sketches(snapshots, range_test, test_rows, block=1024):
    cells, times = snapshots.shape
    rank = range_test.shape[1]
    sketch = test_rows.shape[0]
    return pl.pallas_call(
        sketch_kernel,
        grid=(cells // block,),
        in_specs=[
            pl.BlockSpec((block, times), lambda i: (i, 0)),
            pl.BlockSpec((sketch, block), lambda i: (0, i)),
            pl.BlockSpec((times, rank), lambda i: (0, 0)),
        ],
        out_specs=[
            pl.BlockSpec((rank, block), lambda i: (0, i)),
            pl.BlockSpec((2, times, sketch // 2), lambda i: (0, 0, 0)),
            pl.BlockSpec((sketch + rank, rank), lambda i: (0, 0)),
        ],
        out_shape=[
            jax.ShapeDtypeStruct((rank, cells), F32),
            jax.ShapeDtypeStruct((2, times, sketch // 2), F32),
            jax.ShapeDtypeStruct((sketch + rank, rank), F32),
        ],
        scratch_shapes=[
            pltpu.VMEM((rank, times), BF16),
            pltpu.VMEM((sketch, times), F32),
            pltpu.VMEM((2 * rank, 2 * rank), F32),
        ],
        compiler_params=pltpu.CompilerParams(
            dimension_semantics=("arbitrary",), vmem_limit_bytes=40 * 2**20
        ),
        name="sketches",
    )(snapshots, test_rows, range_test)


def solve_kernel(
    cells_total, owned, crit, mine, range_t, adjoint, species, rates, factors, first, second, augmented, lhs, upper
):
    sketch = mine.shape[2] * 2
    rank = crit.shape[1]
    half = sketch // 2
    ends = -(-owned // 8) * 8
    lhs[...] = jnp.zeros_like(lhs)
    for h in range(2):
        lhs[0:owned, h * half : (h + 1) * half] = mine[h]
        for j in range(2):
            for q in range(2):
                place = sketch + j * 4 + h * 2 + q
                lhs[ends + j : ends + j + 1, h * half + q * 64 : h * half + (q + 1) * 64] = crit[
                    place : place + 1, rank // 2 :
                ]
    projected = crit[0:sketch, :]
    turned = projected.T
    augmented[:, 0:rank] = jnp.dot(turned, projected, precision=HIGH, preferred_element_type=F32)
    augmented[:, rank:] = lax.dot_general(turned, lhs[...], NT, precision=HIGH, preferred_element_type=F32)
    gram = crit[sketch:, :]
    row_id = lax.broadcasted_iota(jnp.int32, (rank, rank), 0)
    col_id = lax.broadcasted_iota(jnp.int32, (rank, rank), 1)
    upper[...] = jnp.where(col_id > row_id, gram.T, gram)

    sub = lax.broadcasted_iota(jnp.int32, (8, 1), 0)
    lane = lax.broadcasted_iota(jnp.int32, (1, rank), 1)
    tiles = rank // 8
    for b in range(tiles):
        rows = slice(8 * b, 8 * b + 8)
        tile, _ = reduced(augmented[rows, :], 8 * b, sub)
        augmented[rows, :] = tile
        for i in range(tiles):
            if i != b:
                eliminate(augmented, i, b, tile)
        tile, roots = reduced(upper[rows, :], 8 * b, sub)
        for i in range(b + 1, tiles):
            eliminate(upper, i, b, tile)
        upper[rows, :] = jnp.where(lane >= 8 * b + sub, roots, 0.0)

    solved = augmented[:, rank:]
    out = jnp.dot(upper[...], solved, precision=HIGH, preferred_element_type=F32) * cells_total**-0.5
    factors[...] = out[:, 0:owned]

    rows_here, width = adjoint.shape
    for r in range(rows_here):
        sums = [jnp.zeros((8, width), F32) for _ in range(2)]
        for t in range(tiles):
            part = range_t[8 * t : 8 * t + 8, r * width : (r + 1) * width]
            for j in range(2):
                sums[j] = sums[j] + part * solved[8 * t : 8 * t + 8, ends + j : ends + j + 1]
        for j in range(2):
            (first if j == 1 else second)[r : r + 1, :] = jnp.sum(sums[j], axis=0, keepdims=True)

    kinds = species[...]
    coupling = jnp.zeros(kinds.shape, F32)
    for kind in range(rates.shape[0]):
        coupling = jnp.where(kinds == kind, rates[kind], coupling)
    coupling = STEP_SIZE * coupling
    value = adjoint[...]
    state = first[...]
    none = jnp.zeros((1, width), F32)
    edge = jnp.zeros((rows_here, 1), F32)
    near = jnp.concatenate([none, value[:-1]], axis=0) + jnp.concatenate([value[1:], none], axis=0)
    near = near + jnp.concatenate([edge, value[:, :-1]], axis=1) + jnp.concatenate([value[:, 1:], edge], axis=1)
    first[...] = value + DIFFUSION * (near - 4.0 * value) + coupling * (1.0 - 3.0 * state * state) * value
    state = second[...]
    second[...] = coupling * (1.0 - 3.0 * state * state)


def reduced(tile, first_col, sub):
    cols = [tile[:, first_col + k : first_col + k + 1] for k in range(8)]
    roots = tile
    for k in range(8):
        pivot = cols[k][k : k + 1, :]
        inverse = 1.0 / pivot
        row = tile[k : k + 1, :]
        scaled = row * inverse
        roots = jnp.where(sub == k, row * lax.rsqrt(pivot), roots)
        tile = jnp.where(sub == k, scaled, tile - cols[k] * scaled)
        for m in range(k + 1, 8):
            value = cols[m][k : k + 1, :] * inverse
            cols[m] = jnp.where(sub == k, value, cols[m] - cols[k] * value)
    return tile, roots


def eliminate(ref, i, b, tile):
    there = slice(8 * i, 8 * i + 8)
    other = ref[there, :]
    cols = [other[:, 8 * b + k : 8 * b + k + 1] for k in range(8)]
    for k in range(8):
        other = other - cols[k] * tile[k : k + 1, :]
    ref[there, :] = other


def solve(crit, mine, range_t, adjoint, species, rates, cells_total):
    owned = mine.shape[1]
    rank = crit.shape[1]
    sketch = 2 * mine.shape[2]
    vmem = pl.BlockSpec(memory_space=pltpu.VMEM)
    return pl.pallas_call(
        functools.partial(solve_kernel, cells_total, owned),
        in_specs=[vmem, vmem, vmem, vmem, vmem, pl.BlockSpec(memory_space=pltpu.SMEM)],
        out_specs=[vmem, vmem, vmem],
        out_shape=[
            jax.ShapeDtypeStruct((rank, owned), F32),
            jax.ShapeDtypeStruct(adjoint.shape, F32),
            jax.ShapeDtypeStruct(adjoint.shape, F32),
        ],
        scratch_shapes=[
            pltpu.VMEM((rank, 2 * rank), F32),
            pltpu.VMEM((rank, sketch), F32),
            pltpu.VMEM((rank, rank), F32),
        ],
        compiler_params=pltpu.CompilerParams(vmem_limit_bytes=40 * 2**20),
        name="solve",
    )(crit, mine, range_t, adjoint, species, rates)


def partners(count, shift, other):
    return [(i, i ^ (other << shift)) for i in range(count)]


def member(shift, size):
    return (lax.axis_index(AXES) >> shift) & (size - 1)


def pick(pieces, index):
    return lax.dynamic_index_in_dim(pieces, index, 0, keepdims=False)


def summed_pieces(pieces, count, shift):
    size = pieces.shape[0]
    me = member(shift, size)
    got = [lax.ppermute(pick(pieces, me ^ p), AXES, partners(count, shift, p)) for p in range(1, size)]
    total = pick(pieces, me)
    for piece in got:
        total = total + piece
    return total


def gathered_pieces(piece, count, shift, size):
    me = member(shift, size)
    got = [lax.ppermute(piece, AXES, partners(count, shift, p)) for p in range(1, size)]
    out = jnp.zeros((size,) + piece.shape, piece.dtype)
    for p, part in enumerate([piece] + got):
        out = lax.dynamic_update_index_in_dim(out, part, me ^ p, 0)
    return out


def stages(count):
    bits = count.bit_length() - 1
    out, shift = [(0, 2)], 1
    while shift < bits:
        width = min(2, bits - shift)
        out.append((shift, 1 << width))
        shift += width
    return out


def reduce_sketches(crit, ct, count):
    plan = stages(count)
    halves, times, width = ct.shape
    owned = times // count
    left = count
    for shift, size in plan[:-1]:
        left //= size
        crit = crit.reshape(size, -1, width)
        ct = ct.reshape(halves, left, size, owned, width)
        ct = jnp.moveaxis(ct, 2, 0).reshape(size, -1, width)
        split = crit.shape[1]
        both = summed_pieces(jnp.concatenate([crit, ct], axis=1), count, shift)
        crit, ct = both[:split], both[split:].reshape(halves, left * owned, width)
    shift, size = plan[-1]
    ct = ct.reshape(halves, size, owned, width)
    ct = jnp.moveaxis(ct, 1, 0).reshape(size, -1, width)
    split = crit.shape[0]
    whole = jnp.broadcast_to(crit[None], (size,) + crit.shape)
    both = summed_pieces(jnp.concatenate([whole, ct], axis=1), count, shift)
    crit, mine = both[:split], both[split:].reshape(halves, owned, width)
    for shift, size in plan[-2::-1]:
        crit = gathered_pieces(crit, count, shift, size).reshape(-1, width)
    return crit, mine


def shards(snapshots, range_test, test_rows, species, reaction_rates, adjoint_end):
    count = lax.axis_size(AXES)
    cells_total = snapshots.shape[0] * count
    range_t, ct, crit = sketches(snapshots, range_test, test_rows)
    crit, mine = reduce_sketches(crit, ct, count)
    time_factors, partial, rate = solve(crit, mine, range_t, adjoint_end, species, reaction_rates, cells_total)
    forward = [(i, i + 1) for i in range(count - 1)]
    backward = [(i + 1, i) for i in range(count - 1)]
    above = lax.ppermute(jnp.concatenate([partial[-1:], adjoint_end[-1:]], axis=0), AXES, forward)
    below = lax.ppermute(jnp.concatenate([partial[:1], adjoint_end[:1]], axis=0), AXES, backward)
    adjoint = jnp.concatenate(
        [partial[:1] + DIFFUSION * above[1:], partial[1:-1], partial[-1:] + DIFFUSION * below[1:]], axis=0
    )
    device = lax.axis_index(AXES)
    top = jnp.where(device > 0, above[:1] + DIFFUSION * adjoint_end[:1], 0.0)
    bottom = jnp.where(device < count - 1, below[:1] + DIFFUSION * adjoint_end[-1:], 0.0)
    padded = jnp.concatenate([top, adjoint, bottom], axis=0)
    sideways = jnp.pad(adjoint, ((0, 0), (1, 1)))
    laplace = padded[2:] + padded[:-2] + sideways[:, 2:] + sideways[:, :-2] - 4.0 * adjoint
    return (adjoint + DIFFUSION * laplace + rate * adjoint, time_factors)


def solution(mesh):
    return jax.shard_map(
        shards,
        mesh=mesh,
        in_specs=(P(AXES, None), P(), P(None, AXES), P(AXES, None), P(), P(AXES, None)),
        out_specs=(P(AXES, None), P(None, AXES)),
        check_vma=False,
    )
```

```python
import functools

import jax
import jax.numpy as jnp
from jax import lax
from jax.experimental import pallas as pl
from jax.experimental.pallas import tpu as pltpu
from jax.sharding import PartitionSpec as P

DIFFUSION = 0.2
STEP_SIZE = 0.05
AXES = ("space", "tm")
HIGH = lax.Precision.HIGHEST
NT = (((1,), (1,)), ((), ()))
F32 = jnp.float32
BF16 = jnp.bfloat16


def sketch_kernel(
    chunks, ahead, snap, test, om, range_out, ct, crit, snap_v, test_v, om_v, range_t, om_t, corange, gram, split, sems
):
    cells, times = snap.shape
    rank = om.shape[1]
    sketch = test.shape[0]
    block = cells // chunks

    def place(i):
        return pl.ds(pl.multiple_of(i * block, block), block)

    def copies(i):
        at = place(i)
        return (
            pltpu.make_async_copy(snap.at[at, :], snap_v.at[at, :], sems.at[2 * i]),
            pltpu.make_async_copy(test.at[:, at], test_v.at[:, at], sems.at[2 * i + 1]),
        )

    def leaving(i):
        return pltpu.make_async_copy(range_t.at[:, place(i)], range_out.at[:, place(i)], sems.at[2 * chunks + 1 + i])

    own = pltpu.make_async_copy(om, om_v, sems.at[2 * chunks])
    own.start()
    for i in range(min(ahead, chunks)):
        for copy in copies(i):
            copy.start()
    corange[...] = jnp.zeros_like(corange)
    gram[...] = jnp.zeros_like(gram)
    split[1] = jnp.zeros(split.shape[1:], BF16)
    own.wait()
    om_t[...] = om_v[...].astype(F32).T.astype(BF16)

    def step(i, carry):
        for copy in copies(i):
            copy.wait()

        @pl.when(i + ahead < chunks)
        def _():
            for copy in copies(i + ahead):
                copy.start()

        at = place(i)
        states = snap_v[at, :]
        before = split[(i + 1) % 2]
        gram[...] += lax.dot_general(before, before, NT, preferred_element_type=F32)
        rt = lax.dot_general(om_t[...], states, NT, preferred_element_type=F32)
        range_t[:, at] = rt
        leaving(i).start()
        upper = rt.astype(BF16)
        split[i % 2, 0:rank] = upper
        split[i % 2, rank:] = (rt - upper.astype(F32)).astype(BF16)
        corange[...] += jnp.dot(test_v[:, at], states, preferred_element_type=F32)
        return carry

    lax.fori_loop(0, chunks, step, 0)
    last = split[(chunks + 1) % 2]
    gram[...] += lax.dot_general(last, last, NT, preferred_element_type=F32)
    whole = corange[...]
    crit[0:sketch, :] = jnp.dot(whole, om_v[...].astype(F32), precision=HIGH, preferred_element_type=F32)
    cross = gram[0:rank, rank:]
    crit[sketch:, :] = gram[0:rank, 0:rank] + cross + cross.T
    half = sketch // 2
    for h in range(2):
        turned = whole[h * half : (h + 1) * half, :].T
        ct[h] = turned
        for j in range(2):
            row = turned[times - 2 + j : times - 1 + j, :]
            for q in range(2):
                there = sketch + j * 4 + h * 2 + q
                crit[there : there + 1, rank // 2 :] = row[:, q * 64 : (q + 1) * 64]
    for i in range(chunks):
        leaving(i).wait()


def sketches(snapshots, range_test, test_rows, chunks=8, ahead=3):
    cells, times = snapshots.shape
    rank = range_test.shape[1]
    sketch = test_rows.shape[0]
    far = pl.BlockSpec(memory_space=pltpu.HBM)
    near = pl.BlockSpec(memory_space=pltpu.VMEM)
    return pl.pallas_call(
        functools.partial(sketch_kernel, chunks, ahead),
        in_specs=[far, far, far],
        out_specs=[far, near, near],
        out_shape=[
            pltpu.HBM((rank, cells), F32),
            jax.ShapeDtypeStruct((2, times, sketch // 2), F32),
            jax.ShapeDtypeStruct((sketch + rank, rank), F32),
        ],
        scratch_shapes=[
            pltpu.VMEM((cells, times), BF16),
            pltpu.VMEM((sketch, cells), BF16),
            pltpu.VMEM((times, rank), BF16),
            pltpu.VMEM((rank, cells), F32),
            pltpu.VMEM((rank, times), BF16),
            pltpu.VMEM((sketch, times), F32),
            pltpu.VMEM((2 * rank, 2 * rank), F32),
            pltpu.VMEM((2, 2 * rank, cells // chunks), BF16),
            pltpu.SemaphoreType.DMA((3 * chunks + 1,)),
        ],
        compiler_params=pltpu.CompilerParams(vmem_limit_bytes=40 * 2**20),
        name="sketches",
    )(*[pltpu.with_memory_space_constraint(x, pltpu.HBM) for x in (snapshots, test_rows, range_test)])


def solve_kernel(
    cells_total, owned, crit, mine, range_in, adjoint, species, rates, factors, first, second,
    augmented, lhs, upper, chol, range_t, sems
):
    pieces = sems.shape[0]
    many = range_in.shape[0] // pieces
    arriving = [
        pltpu.make_async_copy(range_in.at[pl.ds(i * many, many)], range_t.at[pl.ds(i * many, many)], sems.at[i])
        for i in range(pieces)
    ]
    for copy in arriving:
        copy.start()
    sketch = mine.shape[2] * 2
    rank = crit.shape[1]
    half = sketch // 2
    ends = -(-owned // 8) * 8
    lhs[...] = jnp.zeros_like(lhs)
    for h in range(2):
        lhs[0:owned, h * half : (h + 1) * half] = mine[h]
        for j in range(2):
            for q in range(2):
                place = sketch + j * 4 + h * 2 + q
                lhs[ends + j : ends + j + 1, h * half + q * 64 : h * half + (q + 1) * 64] = crit[
                    place : place + 1, rank // 2 :
                ]
    projected = crit[0:sketch, :]
    turned = projected.T
    augmented[:, 0:rank] = jnp.dot(turned, projected, precision=HIGH, preferred_element_type=F32)
    augmented[:, rank:] = lax.dot_general(turned, lhs[...], NT, precision=HIGH, preferred_element_type=F32)
    gram = crit[sketch:, :]
    row_id = lax.broadcasted_iota(jnp.int32, (rank, rank), 0)
    col_id = lax.broadcasted_iota(jnp.int32, (rank, rank), 1)
    upper[...] = jnp.where(col_id > row_id, gram.T, gram)

    sub = lax.broadcasted_iota(jnp.int32, (8, rank), 0)
    lane = lax.broadcasted_iota(jnp.int32, (8, rank), 1)
    tiles = rank // 8
    per = tiles // 2
    size = 8 * per
    for start in range(0, rank, size):
        here = slice(start, start + size)
        left = [[augmented[start + 8 * i : start + 8 * i + 8, :rank], augmented[start + 8 * i : start + 8 * i + 8, rank:]] for i in range(per)]
        right = [[upper[start + 8 * i : start + 8 * i + 8, :]] for i in range(per)]
        for b in range(per):
            at = start + 8 * b
            left[b], _ = reduced(left[b], at, sub)
            right[b], roots = reduced(right[b], at, sub)
            chol[at : at + 8, :] = jnp.where(lane >= at + sub, roots, 0.0)
            for i in range(b + 1, b + per):
                left[i % per] = eliminated(left[i % per], at, left[b])
                right[i % per] = eliminated(right[i % per], at, right[b])
        panel = [jnp.concatenate([row[p] for row in left], axis=0) for p in range(2)]
        panel = jnp.concatenate(panel, axis=1)
        others = [slice(0, start), slice(start + size, rank)]
        taken = jnp.concatenate([augmented[o, :rank] for o in others if o.stop > o.start], axis=0)
        change = jnp.dot(taken, spread(panel, start, rank), precision=HIGH, preferred_element_type=F32)
        done = 0
        for o in others:
            if o.stop > o.start:
                many = o.stop - o.start
                augmented[o, :] = augmented[o, :] - change[done : done + many, :]
                done += many
        augmented[here, :] = panel
        rest = slice(start + size, rank)
        if rest.stop > rest.start:
            panel = jnp.concatenate([row[0] for row in right], axis=0)
            upper[rest, :] = upper[rest, :] - jnp.dot(
                upper[rest, :], spread(panel, start, rank), precision=HIGH, preferred_element_type=F32
            )

    solved = augmented[:, rank:]
    out = jnp.dot(chol[...], solved, precision=HIGH, preferred_element_type=F32) * cells_total**-0.5
    factors[...] = out[:, 0:owned]

    for copy in arriving:
        copy.wait()
    rows_here, width = adjoint.shape
    for r in range(rows_here):
        sums = [jnp.zeros((8, width), F32) for _ in range(2)]
        for t in range(tiles):
            part = range_t[8 * t : 8 * t + 8, r * width : (r + 1) * width]
            for j in range(2):
                sums[j] = sums[j] + part * solved[8 * t : 8 * t + 8, ends + j : ends + j + 1]
        for j in range(2):
            (first if j == 1 else second)[r : r + 1, :] = jnp.sum(sums[j], axis=0, keepdims=True)

    kinds = species[...]
    coupling = jnp.zeros(kinds.shape, F32)
    for kind in range(rates.shape[0]):
        coupling = jnp.where(kinds == kind, rates[kind], coupling)
    coupling = STEP_SIZE * coupling
    value = adjoint[...]
    state = first[...]
    none = jnp.zeros((1, width), F32)
    edge = jnp.zeros((rows_here, 1), F32)
    near = jnp.concatenate([none, value[:-1]], axis=0) + jnp.concatenate([value[1:], none], axis=0)
    near = near + jnp.concatenate([edge, value[:, :-1]], axis=1) + jnp.concatenate([value[:, 1:], edge], axis=1)
    first[...] = value + DIFFUSION * (near - 4.0 * value) + coupling * (1.0 - 3.0 * state * state) * value
    state = second[...]
    second[...] = coupling * (1.0 - 3.0 * state * state)


def spread(panel, first, rank):
    rows = [jnp.zeros((first, panel.shape[1]), F32), panel, jnp.zeros((rank - first - panel.shape[0], panel.shape[1]), F32)]
    return jnp.concatenate([r for r in rows if r.shape[0]], axis=0)


def reduced(tile, first_col, sub):
    block = tile[0].shape
    cols = [jnp.broadcast_to(tile[0][:, first_col + k : first_col + k + 1], block) for k in range(8)]
    roots = tile[0]
    for k in range(8):
        pivot = jnp.broadcast_to(cols[k][k : k + 1, :], block)
        inverse = 1.0 / pivot
        rows = [jnp.broadcast_to(part[k : k + 1, :], block) for part in tile]
        here = sub == k
        roots = jnp.where(here, rows[0] * lax.rsqrt(pivot), roots)
        scaled = [row * inverse for row in rows]
        tile = [jnp.where(here, row, part - cols[k] * row) for row, part in zip(scaled, tile)]
        for m in range(k + 1, 8):
            value = jnp.broadcast_to(cols[m][k : k + 1, :], block) * inverse
            cols[m] = jnp.where(here, value, cols[m] - cols[k] * value)
    return tile, roots


def eliminated(parts, first_col, tile):
    cols = [jnp.broadcast_to(parts[0][:, first_col + k : first_col + k + 1], tile[0].shape) for k in range(8)]
    out = []
    for part, known in zip(parts, tile):
        terms = [cols[k] * jnp.broadcast_to(known[k : k + 1, :], part.shape) for k in range(8)]
        while len(terms) > 1:
            terms = [terms[i] + terms[i + 1] for i in range(0, len(terms), 2)]
        out.append(part - terms[0])
    return out


def solve(crit, mine, range_t, adjoint, species, rates, cells_total):
    owned = mine.shape[1]
    rank = crit.shape[1]
    sketch = 2 * mine.shape[2]
    vmem = pl.BlockSpec(memory_space=pltpu.VMEM)
    return pl.pallas_call(
        functools.partial(solve_kernel, cells_total, owned),
        in_specs=[vmem, vmem, pl.BlockSpec(memory_space=pltpu.HBM), vmem, vmem, pl.BlockSpec(memory_space=pltpu.SMEM)],
        out_specs=[vmem, vmem, vmem],
        out_shape=[
            jax.ShapeDtypeStruct((rank, owned), F32),
            jax.ShapeDtypeStruct(adjoint.shape, F32),
            jax.ShapeDtypeStruct(adjoint.shape, F32),
        ],
        scratch_shapes=[
            pltpu.VMEM((rank, 2 * rank), F32),
            pltpu.VMEM((rank, sketch), F32),
            pltpu.VMEM((rank, rank), F32),
            pltpu.VMEM((rank, rank), F32),
            pltpu.VMEM(range_t.shape, F32),
            pltpu.SemaphoreType.DMA((8,)),
        ],
        compiler_params=pltpu.CompilerParams(vmem_limit_bytes=16 * 2**20),
        name="solve",
    )(crit, mine, pltpu.with_memory_space_constraint(range_t, pltpu.HBM), adjoint, species, rates)


def partners(count, shift, other):
    return [(i, i ^ (other << shift)) for i in range(count)]


def member(shift, size):
    return (lax.axis_index(AXES) >> shift) & (size - 1)


def pick(pieces, index):
    return lax.dynamic_index_in_dim(pieces, index, 0, keepdims=False)


def summed_pieces(pieces, count, shift):
    size = pieces.shape[0]
    me = member(shift, size)
    got = [lax.ppermute(pick(pieces, me ^ p), AXES, partners(count, shift, p)) for p in range(1, size)]
    total = pick(pieces, me)
    for piece in got:
        total = total + piece
    return total


def gathered_pieces(piece, count, shift, size):
    me = member(shift, size)
    got = [lax.ppermute(piece, AXES, partners(count, shift, p)) for p in range(1, size)]
    out = jnp.zeros((size,) + piece.shape, piece.dtype)
    for p, part in enumerate([piece] + got):
        out = lax.dynamic_update_index_in_dim(out, part, me ^ p, 0)
    return out


def stages(count):
    bits = count.bit_length() - 1
    out, shift = [(0, 2)], 1
    while shift < bits:
        width = min(2, bits - shift)
        out.append((shift, 1 << width))
        shift += width
    return out


def reduce_sketches(crit, ct, count):
    plan = stages(count)
    halves, times, width = ct.shape
    owned = times // count
    left = count
    for shift, size in plan[:-1]:
        left //= size
        crit = crit.reshape(size, -1, width)
        ct = ct.reshape(halves, left, size, owned, width)
        ct = jnp.moveaxis(ct, 2, 0).reshape(size, -1, width)
        split = crit.shape[1]
        both = summed_pieces(jnp.concatenate([crit, ct], axis=1), count, shift)
        crit, ct = both[:split], both[split:].reshape(halves, left * owned, width)
    shift, size = plan[-1]
    ct = ct.reshape(halves, size, owned, width)
    ct = jnp.moveaxis(ct, 1, 0).reshape(size, -1, width)
    split = crit.shape[0]
    whole = jnp.broadcast_to(crit[None], (size,) + crit.shape)
    both = summed_pieces(jnp.concatenate([whole, ct], axis=1), count, shift)
    crit, mine = both[:split], both[split:].reshape(halves, owned, width)
    for shift, size in plan[-2::-1]:
        crit = gathered_pieces(crit, count, shift, size).reshape(-1, width)
    return crit, mine


def shards(snapshots, range_test, test_rows, species, reaction_rates, adjoint_end):
    count = lax.axis_size(AXES)
    cells_total = snapshots.shape[0] * count
    range_t, ct, crit = sketches(snapshots, range_test, test_rows)
    crit, mine = reduce_sketches(crit, ct, count)
    time_factors, partial, rate = solve(crit, mine, range_t, adjoint_end, species, reaction_rates, cells_total)
    device = lax.axis_index(AXES)
    even = device % 2 == 0
    head = jnp.concatenate([partial[:1], adjoint_end[:1]], axis=0)
    tail = jnp.concatenate([partial[-1:], adjoint_end[-1:]], axis=0)
    pairs = [(i, i ^ 1) for i in range(count)]
    across = [(i, i + 1) for i in range(1, count - 1, 2)] + [(i + 1, i) for i in range(1, count - 1, 2)]
    far = lax.ppermute(jnp.where(even, head, tail), AXES, across)
    near = lax.ppermute(jnp.where(even, tail, head), AXES, pairs)
    above = jnp.where(even, far, near)
    below = jnp.where(even, near, far)
    adjoint = jnp.concatenate(
        [partial[:1] + DIFFUSION * above[1:], partial[1:-1], partial[-1:] + DIFFUSION * below[1:]], axis=0
    )
    top = jnp.where(device > 0, above[:1] + DIFFUSION * adjoint_end[:1], 0.0)
    bottom = jnp.where(device < count - 1, below[:1] + DIFFUSION * adjoint_end[-1:], 0.0)
    padded = jnp.concatenate([top, adjoint, bottom], axis=0)
    sideways = jnp.pad(adjoint, ((0, 0), (1, 1)))
    laplace = padded[2:] + padded[:-2] + sideways[:, 2:] + sideways[:, :-2] - 4.0 * adjoint
    return (adjoint + DIFFUSION * laplace + rate * adjoint, time_factors)


def solution(mesh):
    return jax.shard_map(
        shards,
        mesh=mesh,
        in_specs=(P(AXES, None), P(), P(None, AXES), P(AXES, None), P(), P(AXES, None)),
        out_specs=(P(AXES, None), P(None, AXES)),
        check_vma=False,
    )
```

```python
import functools

import jax
import jax.numpy as jnp
from jax import lax
from jax.experimental import pallas as pl
from jax.experimental.pallas import tpu as pltpu
from jax.sharding import PartitionSpec as P

DIFFUSION = 0.2
STEP_SIZE = 0.05
AXES = ("space", "tm")
HIGH = lax.Precision.HIGHEST
NT = (((1,), (1,)), ((), ()))
F32 = jnp.float32
BF16 = jnp.bfloat16


def sketch_kernel(
    chunks, ahead, snap, test, om, range_out, ct, crit, snap_v, test_v, om_v, range_t, om_t, corange, gram, split, sems
):
    cells, times = snap.shape
    rank = om.shape[1]
    sketch = test.shape[0]
    block = cells // chunks

    def place(i):
        return pl.ds(pl.multiple_of(i * block, block), block)

    def copies(i):
        at = place(i)
        return (
            pltpu.make_async_copy(snap.at[at, :], snap_v.at[at, :], sems.at[2 * i]),
            pltpu.make_async_copy(test.at[:, at], test_v.at[:, at], sems.at[2 * i + 1]),
        )

    def leaving(i):
        return pltpu.make_async_copy(range_t.at[:, place(i)], range_out.at[:, place(i)], sems.at[2 * chunks + 1 + i])

    own = pltpu.make_async_copy(om, om_v, sems.at[2 * chunks])
    own.start()
    for i in range(min(ahead, chunks)):
        for copy in copies(i):
            copy.start()
    corange[...] = jnp.zeros_like(corange)
    gram[...] = jnp.zeros_like(gram)
    split[1] = jnp.zeros(split.shape[1:], BF16)
    own.wait()
    om_t[...] = om_v[...].astype(F32).T.astype(BF16)

    def step(i, carry):
        for copy in copies(i):
            copy.wait()

        @pl.when(i + ahead < chunks)
        def _():
            for copy in copies(i + ahead):
                copy.start()

        at = place(i)
        states = snap_v[at, :]
        before = split[(i + 1) % 2]
        gram[...] += lax.dot_general(before, before, NT, preferred_element_type=F32)
        rt = lax.dot_general(om_t[...], states, NT, preferred_element_type=F32)
        range_t[:, at] = rt
        leaving(i).start()
        upper = rt.astype(BF16)
        split[i % 2, 0:rank] = upper
        split[i % 2, rank:] = (rt - upper.astype(F32)).astype(BF16)
        corange[...] += jnp.dot(test_v[:, at], states, preferred_element_type=F32)
        return carry

    lax.fori_loop(0, chunks, step, 0)
    last = split[(chunks + 1) % 2]
    gram[...] += lax.dot_general(last, last, NT, preferred_element_type=F32)
    whole = corange[...]
    crit[0:sketch, :] = jnp.dot(whole, om_v[...].astype(F32), precision=HIGH, preferred_element_type=F32)
    cross = gram[0:rank, rank:]
    crit[sketch:, :] = gram[0:rank, 0:rank] + cross + cross.T
    half = sketch // 2
    for h in range(2):
        turned = whole[h * half : (h + 1) * half, :].T
        ct[h] = turned
        for j in range(2):
            row = turned[times - 2 + j : times - 1 + j, :]
            for q in range(2):
                there = sketch + j * 4 + h * 2 + q
                crit[there : there + 1, rank // 2 :] = row[:, q * 64 : (q + 1) * 64]
    for i in range(chunks):
        leaving(i).wait()


def sketches(snapshots, range_test, test_rows, chunks=8, ahead=3):
    cells, times = snapshots.shape
    rank = range_test.shape[1]
    sketch = test_rows.shape[0]
    far = pl.BlockSpec(memory_space=pltpu.HBM)
    near = pl.BlockSpec(memory_space=pltpu.VMEM)
    return pl.pallas_call(
        functools.partial(sketch_kernel, chunks, ahead),
        in_specs=[far, far, far],
        out_specs=[far, near, near],
        out_shape=[
            pltpu.HBM((rank, cells), F32),
            jax.ShapeDtypeStruct((2, times, sketch // 2), F32),
            jax.ShapeDtypeStruct((sketch + rank, rank), F32),
        ],
        scratch_shapes=[
            pltpu.VMEM((cells, times), BF16),
            pltpu.VMEM((sketch, cells), BF16),
            pltpu.VMEM((times, rank), BF16),
            pltpu.VMEM((rank, cells), F32),
            pltpu.VMEM((rank, times), BF16),
            pltpu.VMEM((sketch, times), F32),
            pltpu.VMEM((2 * rank, 2 * rank), F32),
            pltpu.VMEM((2, 2 * rank, cells // chunks), BF16),
            pltpu.SemaphoreType.DMA((3 * chunks + 1,)),
        ],
        compiler_params=pltpu.CompilerParams(vmem_limit_bytes=40 * 2**20),
        name="sketches",
    )(*[pltpu.with_memory_space_constraint(x, pltpu.HBM) for x in (snapshots, test_rows, range_test)])


def solve_kernel(
    cells_total, owned, crit, mine, range_t, adjoint, species, rates, factors, first, second,
    augmented, lhs, upper, chol
):
    sketch = mine.shape[2] * 2
    rank = crit.shape[1]
    half = sketch // 2
    ends = -(-owned // 8) * 8
    lhs[...] = jnp.zeros_like(lhs)
    for h in range(2):
        lhs[0:owned, h * half : (h + 1) * half] = mine[h]
        for j in range(2):
            for q in range(2):
                place = sketch + j * 4 + h * 2 + q
                lhs[ends + j : ends + j + 1, h * half + q * 64 : h * half + (q + 1) * 64] = crit[
                    place : place + 1, rank // 2 :
                ]
    projected = crit[0:sketch, :]
    turned = projected.T
    augmented[:, 0:rank] = jnp.dot(turned, projected, precision=HIGH, preferred_element_type=F32)
    augmented[:, rank:] = lax.dot_general(turned, lhs[...], NT, precision=HIGH, preferred_element_type=F32)
    gram = crit[sketch:, :]
    row_id = lax.broadcasted_iota(jnp.int32, (rank, rank), 0)
    col_id = lax.broadcasted_iota(jnp.int32, (rank, rank), 1)
    upper[...] = jnp.where(col_id > row_id, gram.T, gram)

    sub = lax.broadcasted_iota(jnp.int32, (8, rank), 0)
    lane = lax.broadcasted_iota(jnp.int32, (8, rank), 1)
    tiles = rank // 8
    per = tiles // 2
    size = 8 * per
    for start in range(0, rank, size):
        here = slice(start, start + size)
        left = [[augmented[start + 8 * i : start + 8 * i + 8, :rank], augmented[start + 8 * i : start + 8 * i + 8, rank:]] for i in range(per)]
        right = [[upper[start + 8 * i : start + 8 * i + 8, :]] for i in range(per)]
        for b in range(per):
            at = start + 8 * b
            left[b], _ = reduced(left[b], at, sub)
            right[b], roots = reduced(right[b], at, sub)
            chol[at : at + 8, :] = jnp.where(lane >= at + sub, roots, 0.0)
            for i in range(b + 1, b + per):
                left[i % per] = eliminated(left[i % per], at, left[b])
                right[i % per] = eliminated(right[i % per], at, right[b])
        panel = [jnp.concatenate([row[p] for row in left], axis=0) for p in range(2)]
        panel = jnp.concatenate(panel, axis=1)
        others = [slice(0, start), slice(start + size, rank)]
        taken = jnp.concatenate([augmented[o, :rank] for o in others if o.stop > o.start], axis=0)
        change = jnp.dot(taken, spread(panel, start, rank), precision=HIGH, preferred_element_type=F32)
        done = 0
        for o in others:
            if o.stop > o.start:
                many = o.stop - o.start
                augmented[o, :] = augmented[o, :] - change[done : done + many, :]
                done += many
        augmented[here, :] = panel
        rest = slice(start + size, rank)
        if rest.stop > rest.start:
            panel = jnp.concatenate([row[0] for row in right], axis=0)
            upper[rest, :] = upper[rest, :] - jnp.dot(
                upper[rest, :], spread(panel, start, rank), precision=HIGH, preferred_element_type=F32
            )

    solved = augmented[:, rank:]
    out = jnp.dot(chol[...], solved, precision=HIGH, preferred_element_type=F32) * cells_total**-0.5
    factors[...] = out.T[0:owned]

    rows_here, width = adjoint.shape
    for r in range(rows_here):
        sums = [jnp.zeros((8, width), F32) for _ in range(2)]
        for t in range(tiles):
            part = range_t[8 * t : 8 * t + 8, r * width : (r + 1) * width]
            for j in range(2):
                sums[j] = sums[j] + part * solved[8 * t : 8 * t + 8, ends + j : ends + j + 1]
        for j in range(2):
            (first if j == 1 else second)[r : r + 1, :] = jnp.sum(sums[j], axis=0, keepdims=True)

    kinds = species[...]
    coupling = jnp.zeros(kinds.shape, F32)
    for kind in range(rates.shape[0]):
        coupling = jnp.where(kinds == kind, rates[kind], coupling)
    coupling = STEP_SIZE * coupling
    value = adjoint[...]
    state = first[...]
    none = jnp.zeros((1, width), F32)
    edge = jnp.zeros((rows_here, 1), F32)
    near = jnp.concatenate([none, value[:-1]], axis=0) + jnp.concatenate([value[1:], none], axis=0)
    near = near + jnp.concatenate([edge, value[:, :-1]], axis=1) + jnp.concatenate([value[:, 1:], edge], axis=1)
    first[...] = value + DIFFUSION * (near - 4.0 * value) + coupling * (1.0 - 3.0 * state * state) * value
    state = second[...]
    second[...] = coupling * (1.0 - 3.0 * state * state)


def spread(panel, first, rank):
    rows = [jnp.zeros((first, panel.shape[1]), F32), panel, jnp.zeros((rank - first - panel.shape[0], panel.shape[1]), F32)]
    return jnp.concatenate([r for r in rows if r.shape[0]], axis=0)


def reduced(tile, first_col, sub):
    block = tile[0].shape
    cols = [jnp.broadcast_to(tile[0][:, first_col + k : first_col + k + 1], block) for k in range(8)]
    roots = tile[0]
    for k in range(8):
        pivot = jnp.broadcast_to(cols[k][k : k + 1, :], block)
        inverse = 1.0 / pivot
        rows = [jnp.broadcast_to(part[k : k + 1, :], block) for part in tile]
        here = sub == k
        roots = jnp.where(here, rows[0] * lax.rsqrt(pivot), roots)
        scaled = [row * inverse for row in rows]
        tile = [jnp.where(here, row, part - cols[k] * row) for row, part in zip(scaled, tile)]
        for m in range(k + 1, 8):
            value = jnp.broadcast_to(cols[m][k : k + 1, :], block) * inverse
            cols[m] = jnp.where(here, value, cols[m] - cols[k] * value)
    return tile, roots


def eliminated(parts, first_col, tile):
    cols = [jnp.broadcast_to(parts[0][:, first_col + k : first_col + k + 1], tile[0].shape) for k in range(8)]
    out = []
    for part, known in zip(parts, tile):
        terms = [cols[k] * jnp.broadcast_to(known[k : k + 1, :], part.shape) for k in range(8)]
        while len(terms) > 1:
            terms = [terms[i] + terms[i + 1] for i in range(0, len(terms), 2)]
        out.append(part - terms[0])
    return out


def fetch_kernel(source, out, sems):
    pieces = sems.shape[0]
    many = source.shape[0] // pieces
    copies = [
        pltpu.make_async_copy(source.at[pl.ds(i * many, many)], out.at[pl.ds(i * many, many)], sems.at[i])
        for i in range(pieces)
    ]
    for copy in copies:
        copy.start()
    for copy in copies:
        copy.wait()


def fetch(array):
    return pl.pallas_call(
        fetch_kernel,
        in_specs=[pl.BlockSpec(memory_space=pltpu.HBM)],
        out_specs=pl.BlockSpec(memory_space=pltpu.VMEM),
        out_shape=jax.ShapeDtypeStruct(array.shape, array.dtype),
        scratch_shapes=[pltpu.SemaphoreType.DMA((8,))],
        compiler_params=pltpu.CompilerParams(vmem_limit_bytes=2**20),
        cost_estimate=pl.CostEstimate(flops=0, bytes_accessed=8 * array.size, transcendentals=0),
        name="fetch",
    )(pltpu.with_memory_space_constraint(array, pltpu.HBM))


def solve(crit, mine, range_t, adjoint, species, rates, cells_total):
    owned = mine.shape[1]
    rank = crit.shape[1]
    sketch = 2 * mine.shape[2]
    vmem = pl.BlockSpec(memory_space=pltpu.VMEM)
    return pl.pallas_call(
        functools.partial(solve_kernel, cells_total, owned),
        in_specs=[vmem, vmem, vmem, vmem, vmem, pl.BlockSpec(memory_space=pltpu.SMEM)],
        out_specs=[vmem, vmem, vmem],
        out_shape=[
            jax.ShapeDtypeStruct((owned, rank), F32),
            jax.ShapeDtypeStruct(adjoint.shape, F32),
            jax.ShapeDtypeStruct(adjoint.shape, F32),
        ],
        scratch_shapes=[
            pltpu.VMEM((rank, 2 * rank), F32),
            pltpu.VMEM((rank, sketch), F32),
            pltpu.VMEM((rank, rank), F32),
            pltpu.VMEM((rank, rank), F32),
        ],
        compiler_params=pltpu.CompilerParams(vmem_limit_bytes=16 * 2**20),
        name="solve",
    )(crit, mine, range_t, adjoint, species, rates)


def partners(count, shift, other):
    return [(i, i ^ (other << shift)) for i in range(count)]


def member(shift, size):
    return (lax.axis_index(AXES) >> shift) & (size - 1)


def pick(pieces, index):
    return lax.dynamic_index_in_dim(pieces, index, 0, keepdims=False)


def summed_pieces(pieces, count, shift):
    size = pieces.shape[0]
    me = member(shift, size)
    got = [lax.ppermute(pick(pieces, me ^ p), AXES, partners(count, shift, p)) for p in range(1, size)]
    total = pick(pieces, me)
    for piece in got:
        total = total + piece
    return total


def gathered_pieces(piece, count, shift, size):
    me = member(shift, size)
    got = [lax.ppermute(piece, AXES, partners(count, shift, p)) for p in range(1, size)]
    out = jnp.zeros((size,) + piece.shape, piece.dtype)
    for p, part in enumerate([piece] + got):
        out = lax.dynamic_update_index_in_dim(out, part, me ^ p, 0)
    return out


def stages(count):
    bits = count.bit_length() - 1
    out, shift = [(0, 2)], 1
    while shift < bits:
        width = min(2, bits - shift)
        out.append((shift, 1 << width))
        shift += width
    return out


def reduce_sketches(crit, ct, range_t, count):
    plan = stages(count)
    halves, times, width = ct.shape
    owned = times // count
    left = count
    for shift, size in plan[:-1]:
        left //= size
        crit = crit.reshape(size, -1, width)
        ct = ct.reshape(halves, left, size, owned, width)
        ct = jnp.moveaxis(ct, 2, 0).reshape(size, -1, width)
        split = crit.shape[1]
        both = summed_pieces(jnp.concatenate([crit, ct], axis=1), count, shift)
        crit, ct = both[:split], both[split:].reshape(halves, left * owned, width)
    shift, size = plan[-1]
    crit, ct, range_t = lax.optimization_barrier((crit, ct, range_t))
    range_t = fetch(range_t)
    ct = ct.reshape(halves, size, owned, width)
    ct = jnp.moveaxis(ct, 1, 0).reshape(size, -1, width)
    split = crit.shape[0]
    whole = jnp.broadcast_to(crit[None], (size,) + crit.shape)
    both = summed_pieces(jnp.concatenate([whole, ct], axis=1), count, shift)
    crit, mine = both[:split], both[split:].reshape(halves, owned, width)
    for shift, size in plan[-2::-1]:
        crit = gathered_pieces(crit, count, shift, size).reshape(-1, width)
    return crit, mine, range_t


def shards(snapshots, range_test, test_rows, species, reaction_rates, adjoint_end):
    count = lax.axis_size(AXES)
    cells_total = snapshots.shape[0] * count
    range_t, ct, crit = sketches(snapshots, range_test, test_rows)
    crit, mine, range_t = reduce_sketches(crit, ct, range_t, count)
    time_factors, partial, rate = solve(crit, mine, range_t, adjoint_end, species, reaction_rates, cells_total)
    device = lax.axis_index(AXES)
    even = device % 2 == 0
    head = jnp.concatenate([partial[:1], adjoint_end[:1]], axis=0)
    tail = jnp.concatenate([partial[-1:], adjoint_end[-1:]], axis=0)
    pairs = [(i, i ^ 1) for i in range(count)]
    across = [(i, i + 1) for i in range(1, count - 1, 2)] + [(i + 1, i) for i in range(1, count - 1, 2)]
    far = lax.ppermute(jnp.where(even, head, tail), AXES, across)
    near = lax.ppermute(jnp.where(even, tail, head), AXES, pairs)
    above = jnp.where(even, far, near)
    below = jnp.where(even, near, far)
    adjoint = jnp.concatenate(
        [partial[:1] + DIFFUSION * above[1:], partial[1:-1], partial[-1:] + DIFFUSION * below[1:]], axis=0
    )
    top = jnp.where(device > 0, above[:1] + DIFFUSION * adjoint_end[:1], 0.0)
    bottom = jnp.where(device < count - 1, below[:1] + DIFFUSION * adjoint_end[-1:], 0.0)
    padded = jnp.concatenate([top, adjoint, bottom], axis=0)
    sideways = jnp.pad(adjoint, ((0, 0), (1, 1)))
    laplace = padded[2:] + padded[:-2] + sideways[:, 2:] + sideways[:, :-2] - 4.0 * adjoint
    return (adjoint + DIFFUSION * laplace + rate * adjoint, time_factors.T)


def solution(mesh):
    return jax.shard_map(
        shards,
        mesh=mesh,
        in_specs=(P(AXES, None), P(), P(None, AXES), P(AXES, None), P(), P(AXES, None)),
        out_specs=(P(AXES, None), P(None, AXES)),
        check_vma=False,
    )
```

```python
import functools

import jax
import jax.numpy as jnp
from jax import lax
from jax.experimental import pallas as pl
from jax.experimental.pallas import tpu as pltpu
from jax.sharding import PartitionSpec as P

DIFFUSION = 0.2
STEP_SIZE = 0.05
AXES = ("space", "tm")
ROWS = 16
HIGH = lax.Precision.HIGHEST
NT = (((1,), (1,)), ((), ()))
F32 = jnp.float32
BF16 = jnp.bfloat16


def sketch_kernel(
    chunks, ahead, snap, test, om, range_out, ct, crit, snap_v, test_v, om_v, range_t, om_t, corange, gram, split, sems
):
    cells, times = snap.shape
    rank = om.shape[1]
    sketch = test.shape[0]
    block = cells // chunks

    def place(i):
        return pl.ds(pl.multiple_of(i * block, block), block)

    def copies(i):
        at = place(i)
        return (
            pltpu.make_async_copy(snap.at[at, :], snap_v.at[at, :], sems.at[2 * i]),
            pltpu.make_async_copy(test.at[:, at], test_v.at[:, at], sems.at[2 * i + 1]),
        )

    def leaving(i):
        return pltpu.make_async_copy(range_t.at[:, place(i)], range_out.at[:, place(i)], sems.at[2 * chunks + 1 + i])

    own = pltpu.make_async_copy(om, om_v, sems.at[2 * chunks])
    own.start()
    for i in range(min(ahead, chunks)):
        for copy in copies(i):
            copy.start()
    corange[...] = jnp.zeros_like(corange)
    gram[...] = jnp.zeros_like(gram)
    split[1] = jnp.zeros(split.shape[1:], BF16)
    own.wait()
    om_t[...] = om_v[...].astype(F32).T.astype(BF16)

    def step(i, carry):
        for copy in copies(i):
            copy.wait()

        @pl.when(i + ahead < chunks)
        def _():
            for copy in copies(i + ahead):
                copy.start()

        at = place(i)
        states = snap_v[at, :]
        before = split[(i + 1) % 2]
        gram[...] += lax.dot_general(before, before, NT, preferred_element_type=F32)
        rt = lax.dot_general(om_t[...], states, NT, preferred_element_type=F32)
        range_t[:, at] = rt
        leaving(i).start()
        upper = rt.astype(BF16)
        split[i % 2, 0:rank] = upper
        split[i % 2, rank:] = (rt - upper.astype(F32)).astype(BF16)
        corange[...] += jnp.dot(test_v[:, at], states, preferred_element_type=F32)
        return carry

    lax.fori_loop(0, chunks, step, 0)
    last = split[(chunks + 1) % 2]
    gram[...] += lax.dot_general(last, last, NT, preferred_element_type=F32)
    whole = corange[...]
    crit[0:sketch, :] = jnp.dot(whole, om_v[...].astype(F32), precision=HIGH, preferred_element_type=F32)
    cross = gram[0:rank, rank:]
    crit[sketch:, :] = gram[0:rank, 0:rank] + cross + cross.T
    half = sketch // 2
    for h in range(2):
        turned = whole[h * half : (h + 1) * half, :].T
        ct[h] = turned
        for j in range(2):
            row = turned[times - 2 + j : times - 1 + j, :]
            for q in range(2):
                there = sketch + j * 4 + h * 2 + q
                crit[there : there + 1, rank // 2 :] = row[:, q * 64 : (q + 1) * 64]
    for i in range(chunks):
        leaving(i).wait()


def sketches(snapshots, range_test, test_rows, chunks=8, ahead=3):
    cells, times = snapshots.shape
    rank = range_test.shape[1]
    sketch = test_rows.shape[0]
    far = pl.BlockSpec(memory_space=pltpu.HBM)
    near = pl.BlockSpec(memory_space=pltpu.VMEM)
    return pl.pallas_call(
        functools.partial(sketch_kernel, chunks, ahead),
        in_specs=[far, far, far],
        out_specs=[far, near, near],
        out_shape=[
            pltpu.HBM((rank, cells), F32),
            jax.ShapeDtypeStruct((2, times, sketch // 2), F32),
            jax.ShapeDtypeStruct((sketch + rank, rank), F32),
        ],
        scratch_shapes=[
            pltpu.VMEM((cells, times), BF16),
            pltpu.VMEM((sketch, cells), BF16),
            pltpu.VMEM((times, rank), BF16),
            pltpu.VMEM((rank, cells), F32),
            pltpu.VMEM((rank, times), BF16),
            pltpu.VMEM((sketch, times), F32),
            pltpu.VMEM((2 * rank, 2 * rank), F32),
            pltpu.VMEM((2, 2 * rank, cells // chunks), BF16),
            pltpu.SemaphoreType.DMA((3 * chunks + 1,)),
        ],
        compiler_params=pltpu.CompilerParams(vmem_limit_bytes=40 * 2**20),
        name="sketches",
    )(*[pltpu.with_memory_space_constraint(x, pltpu.HBM) for x in (snapshots, test_rows, range_test)])


def solve_kernel(
    cells_total, owned, crit, mine, range_t, adjoint, species, rates, factors, first, second,
    augmented, lhs, upper, chol
):
    sketch = mine.shape[2] * 2
    rank = crit.shape[1]
    half = sketch // 2
    ends = -(-owned // 8) * 8
    lhs[...] = jnp.zeros_like(lhs)
    for h in range(2):
        lhs[0:owned, h * half : (h + 1) * half] = mine[h]
        for j in range(2):
            for q in range(2):
                place = sketch + j * 4 + h * 2 + q
                lhs[ends + j : ends + j + 1, h * half + q * 64 : h * half + (q + 1) * 64] = crit[
                    place : place + 1, rank // 2 :
                ]
    projected = crit[0:sketch, :]
    turned = projected.T
    augmented[:, 0:rank] = jnp.dot(turned, projected, precision=HIGH, preferred_element_type=F32)
    augmented[:, rank:] = lax.dot_general(turned, lhs[...], NT, precision=HIGH, preferred_element_type=F32)
    gram = crit[sketch:, :]
    row_id = lax.broadcasted_iota(jnp.int32, (rank, rank), 0)
    col_id = lax.broadcasted_iota(jnp.int32, (rank, rank), 1)
    upper[...] = jnp.where(col_id > row_id, gram.T, gram)

    many = ROWS
    sub = lax.broadcasted_iota(jnp.int32, (many, rank), 0)
    lane = lax.broadcasted_iota(jnp.int32, (many, rank), 1)
    tiles = rank // 8
    size = rank // 2
    per = size // many
    for start in range(0, rank, size):
        left, right = [], []
        for i in range(per):
            rows = slice(start + many * i, start + many * (i + 1))
            left.append([augmented[rows, :rank], augmented[rows, rank:]])
            right.append([upper[rows, :]])
        for b in range(per):
            at = start + many * b
            left[b], _ = reduced(left[b], at, sub, False)
            right[b], roots = reduced(right[b], at, sub, True)
            chol[at : at + many, :] = jnp.where(lane >= at + sub, roots, 0.0)
            for i in range(b + 1, b + per):
                left[i % per] = eliminated(left[i % per], at, left[b])
            for i in range(b + 1, per):
                right[i] = eliminated(right[i], at, right[b])
            for i in range(b):
                right[i] = eliminated(right[i], at, right[b])
        panel = [jnp.concatenate([row[p] for row in left], axis=0) for p in range(2)]
        ahead = slice(0 if start + size < rank else rank, 2 * rank)
        panel = jnp.concatenate(panel, axis=1)[:, ahead]
        others = [o for o in (slice(0, start), slice(start + size, rank)) if o.stop > o.start]
        taken = jnp.concatenate([augmented[o, :rank] for o in others], axis=0)
        change = jnp.dot(taken, spread(panel, start, rank), precision=HIGH, preferred_element_type=F32)
        done = 0
        for o in others:
            count = o.stop - o.start
            augmented[o, ahead] = augmented[o, ahead] - change[done : done + count, :]
            done += count
        augmented[start : start + size, ahead] = panel
        rest = slice(start + size, rank)
        if rest.stop > rest.start:
            panel = jnp.concatenate([row[0] for row in right], axis=0)
            upper[rest, :] = upper[rest, :] - jnp.dot(
                upper[rest, :], spread(panel, start, rank), precision=HIGH, preferred_element_type=F32
            )

    solved = augmented[:, rank:]
    out = jnp.dot(chol[...], solved, precision=HIGH, preferred_element_type=F32)
    factors[...] = out[:, 0:owned] * cells_total**-0.5

    rows_here, width = adjoint.shape
    for r in range(rows_here):
        sums = [jnp.zeros((8, width), F32) for _ in range(2)]
        for t in range(tiles):
            part = range_t[8 * t : 8 * t + 8, r * width : (r + 1) * width]
            for j in range(2):
                sums[j] = sums[j] + part * solved[8 * t : 8 * t + 8, ends + j : ends + j + 1]
        for j in range(2):
            (first if j == 1 else second)[r : r + 1, :] = jnp.sum(sums[j], axis=0, keepdims=True)

    kinds = species[...]
    coupling = jnp.zeros(kinds.shape, F32)
    for kind in range(rates.shape[0]):
        coupling = jnp.where(kinds == kind, rates[kind], coupling)
    coupling = STEP_SIZE * coupling
    value = adjoint[...]
    state = first[...]
    none = jnp.zeros((1, width), F32)
    edge = jnp.zeros((rows_here, 1), F32)
    near = jnp.concatenate([none, value[:-1]], axis=0) + jnp.concatenate([value[1:], none], axis=0)
    near = near + jnp.concatenate([edge, value[:, :-1]], axis=1) + jnp.concatenate([value[:, 1:], edge], axis=1)
    first[...] = value + DIFFUSION * (near - 4.0 * value) + coupling * (1.0 - 3.0 * state * state) * value
    state = second[...]
    second[...] = coupling * (1.0 - 3.0 * state * state)


def spread(panel, first, rank):
    rows = [jnp.zeros((first, panel.shape[1]), F32), panel, jnp.zeros((rank - first - panel.shape[0], panel.shape[1]), F32)]
    return jnp.concatenate([r for r in rows if r.shape[0]], axis=0)


def reduced(tile, first_col, sub, want_roots):
    block = tile[0].shape
    cols = [jnp.broadcast_to(tile[0][:, first_col + k : first_col + k + 1], block) for k in range(block[0])]
    roots = tile[0]
    for k in range(block[0]):
        pivot = jnp.broadcast_to(cols[k][k : k + 1, :], block)
        inverse = 1.0 / pivot
        rows = [jnp.broadcast_to(part[k : k + 1, :], block) for part in tile]
        here = sub == k
        if want_roots:
            roots = jnp.where(here, rows[0] * lax.rsqrt(pivot), roots)
        scaled = [row * inverse for row in rows]
        tile = [jnp.where(here, row, part - cols[k] * row) for row, part in zip(scaled, tile)]
        for m in range(k + 1, block[0]):
            value = jnp.broadcast_to(cols[m][k : k + 1, :], block) * inverse
            cols[m] = jnp.where(here, value, cols[m] - cols[k] * value)
    return tile, roots


def eliminated(parts, first_col, tile):
    block = tile[0].shape
    cols = [jnp.broadcast_to(parts[0][:, first_col + k : first_col + k + 1], block) for k in range(block[0])]
    out = []
    for part, known in zip(parts, tile):
        terms = [cols[k] * jnp.broadcast_to(known[k : k + 1, :], block) for k in range(block[0])]
        while len(terms) > 1:
            terms = [terms[i] + terms[i + 1] for i in range(0, len(terms), 2)]
        out.append(part - terms[0])
    return out


def fetch_kernel(source, out, sems):
    pieces = sems.shape[0]
    many = source.shape[0] // pieces
    copies = [
        pltpu.make_async_copy(source.at[pl.ds(i * many, many)], out.at[pl.ds(i * many, many)], sems.at[i])
        for i in range(pieces)
    ]
    for copy in copies:
        copy.start()
    for copy in copies:
        copy.wait()


def fetch(array):
    return pl.pallas_call(
        fetch_kernel,
        in_specs=[pl.BlockSpec(memory_space=pltpu.HBM)],
        out_specs=pl.BlockSpec(memory_space=pltpu.VMEM),
        out_shape=jax.ShapeDtypeStruct(array.shape, array.dtype),
        scratch_shapes=[pltpu.SemaphoreType.DMA((8,))],
        compiler_params=pltpu.CompilerParams(vmem_limit_bytes=2**20),
        cost_estimate=pl.CostEstimate(flops=0, bytes_accessed=8 * array.size, transcendentals=0),
        name="fetch",
    )(pltpu.with_memory_space_constraint(array, pltpu.HBM))


def solve(crit, mine, range_t, adjoint, species, rates, cells_total):
    owned = mine.shape[1]
    rank = crit.shape[1]
    sketch = 2 * mine.shape[2]
    vmem = pl.BlockSpec(memory_space=pltpu.VMEM)
    return pl.pallas_call(
        functools.partial(solve_kernel, cells_total, owned),
        in_specs=[vmem, vmem, vmem, vmem, vmem, pl.BlockSpec(memory_space=pltpu.SMEM)],
        out_specs=[vmem, vmem, vmem],
        out_shape=[
            jax.ShapeDtypeStruct((rank, owned), F32),
            jax.ShapeDtypeStruct(adjoint.shape, F32),
            jax.ShapeDtypeStruct(adjoint.shape, F32),
        ],
        scratch_shapes=[
            pltpu.VMEM((rank, 2 * rank), F32),
            pltpu.VMEM((rank, sketch), F32),
            pltpu.VMEM((rank, rank), F32),
            pltpu.VMEM((rank, rank), F32),
        ],
        compiler_params=pltpu.CompilerParams(vmem_limit_bytes=16 * 2**20),
        name="solve",
    )(crit, mine, range_t, adjoint, species, rates)


def partners(count, shift, other):
    return [(i, i ^ (other << shift)) for i in range(count)]


def member(shift, size):
    return (lax.axis_index(AXES) >> shift) & (size - 1)


def pick(pieces, index):
    return lax.dynamic_index_in_dim(pieces, index, 0, keepdims=False)


def summed_pieces(pieces, count, shift):
    size = pieces.shape[0]
    me = member(shift, size)
    got = [lax.ppermute(pick(pieces, me ^ p), AXES, partners(count, shift, p)) for p in range(size - 1, 0, -1)]
    total = pick(pieces, me)
    for piece in got:
        total = total + piece
    return total


def gathered_pieces(piece, count, shift, size):
    me = member(shift, size)
    got = [lax.ppermute(piece, AXES, partners(count, shift, p)) for p in range(size - 1, 0, -1)]
    out = jnp.zeros((size,) + piece.shape, piece.dtype)
    for p, part in zip([0] + list(range(size - 1, 0, -1)), [piece] + got):
        out = lax.dynamic_update_index_in_dim(out, part, me ^ p, 0)
    return out


def stages(count):
    bits = count.bit_length() - 1
    out, shift = [(0, 2)], 1
    while shift < bits:
        width = min(2, bits - shift)
        out.append((shift, 1 << width))
        shift += width
    return out


def reduce_sketches(crit, ct, range_t, count):
    plan = stages(count)
    halves, times, width = ct.shape
    owned = times // count
    left = count
    for shift, size in plan[:-1]:
        left //= size
        crit = crit.reshape(size, -1, width)
        ct = ct.reshape(halves, left, size, owned, width)
        ct = jnp.moveaxis(ct, 2, 0).reshape(size, -1, width)
        split = crit.shape[1]
        both = summed_pieces(jnp.concatenate([crit, ct], axis=1), count, shift)
        crit, ct = both[:split], both[split:].reshape(halves, left * owned, width)
    shift, size = plan[-1]
    crit, ct, range_t = lax.optimization_barrier((crit, ct, range_t))
    range_t = fetch(range_t)
    ct = ct.reshape(halves, size, owned, width)
    ct = jnp.moveaxis(ct, 1, 0).reshape(size, -1, width)
    split = crit.shape[0]
    whole = jnp.broadcast_to(crit[None], (size,) + crit.shape)
    both = summed_pieces(jnp.concatenate([whole, ct], axis=1), count, shift)
    crit, mine = both[:split], both[split:].reshape(halves, owned, width)
    for shift, size in plan[-2::-1]:
        crit = gathered_pieces(crit, count, shift, size).reshape(-1, width)
    return crit, mine, range_t


def shards(snapshots, range_test, test_rows, species, reaction_rates, adjoint_end):
    count = lax.axis_size(AXES)
    cells_total = snapshots.shape[0] * count
    range_t, ct, crit = sketches(snapshots, range_test, test_rows)
    crit, mine, range_t = reduce_sketches(crit, ct, range_t, count)
    time_factors, partial, rate = solve(crit, mine, range_t, adjoint_end, species, reaction_rates, cells_total)
    device = lax.axis_index(AXES)
    even = device % 2 == 0
    head = jnp.concatenate([partial[:1], adjoint_end[:1]], axis=0)
    tail = jnp.concatenate([partial[-1:], adjoint_end[-1:]], axis=0)
    pairs = [(i, i ^ 1) for i in range(count)]
    across = [(i, i + 1) for i in range(1, count - 1, 2)] + [(i + 1, i) for i in range(1, count - 1, 2)]
    far = lax.ppermute(jnp.where(even, head, tail), AXES, across)
    near = lax.ppermute(jnp.where(even, tail, head), AXES, pairs)
    above = jnp.where(even, far, near)
    below = jnp.where(even, near, far)
    adjoint = jnp.concatenate(
        [partial[:1] + DIFFUSION * above[1:], partial[1:-1], partial[-1:] + DIFFUSION * below[1:]], axis=0
    )
    top = jnp.where(device > 0, above[:1] + DIFFUSION * adjoint_end[:1], 0.0)
    bottom = jnp.where(device < count - 1, below[:1] + DIFFUSION * adjoint_end[-1:], 0.0)
    padded = jnp.concatenate([top, adjoint, bottom], axis=0)
    sideways = jnp.pad(adjoint, ((0, 0), (1, 1)))
    laplace = padded[2:] + padded[:-2] + sideways[:, 2:] + sideways[:, :-2] - 4.0 * adjoint
    return (adjoint + DIFFUSION * laplace + rate * adjoint, time_factors)


def solution(mesh):
    return jax.shard_map(
        shards,
        mesh=mesh,
        in_specs=(P(AXES, None), P(), P(None, AXES), P(AXES, None), P(), P(AXES, None)),
        out_specs=(P(AXES, None), P(None, AXES)),
        check_vma=False,
    )
```

```python
import functools

import jax
import jax.numpy as jnp
from jax import lax
from jax.experimental import pallas as pl
from jax.experimental.pallas import tpu as pltpu
from jax.sharding import PartitionSpec as P

DIFFUSION = 0.2
STEP_SIZE = 0.05
AXES = ("space", "tm")
ROWS = 16
HIGH = lax.Precision.HIGHEST
NT = (((1,), (1,)), ((), ()))
F32 = jnp.float32
BF16 = jnp.bfloat16


def sketch_kernel(
    sizes, ahead, snap, test, om, range_out, ct, crit,
    snap_v, test_v, om_v, range_t, om_t, corange, gram, split, sems,
):
    times = snap.shape[1]
    rank = om.shape[1]
    sketch = test.shape[0]
    blocks = len(sizes)
    places = [pl.ds(sum(sizes[:i]), sizes[i]) for i in range(blocks)]

    def copies(i):
        at = places[i]
        return (
            pltpu.make_async_copy(snap.at[at, :], snap_v.at[at, :], sems.at[2 * i]),
            pltpu.make_async_copy(test.at[:, at], test_v.at[:, at], sems.at[2 * i + 1]),
        )

    def leaving(i):
        return pltpu.make_async_copy(range_t.at[:, places[i]], range_out.at[:, places[i]], sems.at[2 * blocks + 1 + i])

    def gram_of(i):
        part = split[:, places[i]]
        return lax.dot_general(part, part, NT, preferred_element_type=F32)

    own = pltpu.make_async_copy(om, om_v, sems.at[2 * blocks])
    own.start()
    for i in range(min(ahead, blocks)):
        for copy in copies(i):
            copy.start()
    corange[...] = jnp.zeros_like(corange)
    gram[...] = jnp.zeros_like(gram)
    own.wait()
    om_t[...] = om_v[...].astype(F32).T.astype(BF16)
    for i in range(blocks):
        for copy in copies(i):
            copy.wait()
        if i + ahead < blocks:
            for copy in copies(i + ahead):
                copy.start()
        at = places[i]
        states = snap_v[at, :]
        if i:
            gram[...] += gram_of(i - 1)
        rt = lax.dot_general(om_t[...], states, NT, preferred_element_type=F32)
        range_t[:, at] = rt
        leaving(i).start()
        upper = rt.astype(BF16)
        split[0:rank, at] = upper
        split[rank:, at] = (rt - upper.astype(F32)).astype(BF16)
        corange[...] += jnp.dot(test_v[:, at], states, preferred_element_type=F32)
    gram[...] += gram_of(blocks - 1)
    whole = corange[...]
    high = whole.astype(BF16)
    rest = whole - high.astype(F32)
    middle = rest.astype(BF16)
    low = (rest - middle.astype(F32)).astype(BF16)
    projected = jnp.zeros((sketch, rank), F32)
    for part in (low, middle, high):
        projected = projected + jnp.dot(part, om_v[...], preferred_element_type=F32)
    crit[0:sketch, :] = projected
    cross = gram[0:rank, rank:]
    crit[sketch:, :] = gram[0:rank, 0:rank] + cross + cross.T
    half = sketch // 2
    for h in range(2):
        turned = whole[h * half : (h + 1) * half, :].T
        ct[h] = turned
        for j in range(2):
            row = turned[times - 2 + j : times - 1 + j, :]
            for q in range(2):
                there = sketch + j * 4 + h * 2 + q
                crit[there : there + 1, rank // 2 :] = row[:, q * 64 : (q + 1) * 64]
    for i in range(blocks):
        leaving(i).wait()


def sketches(snapshots, range_test, test_rows, shares=(1, 1, 2, 2, 2), ahead=3):
    cells, times = snapshots.shape
    rank = range_test.shape[1]
    sketch = test_rows.shape[0]
    sizes = [share * cells // sum(shares) for share in shares]
    far = pl.BlockSpec(memory_space=pltpu.HBM)
    near = pl.BlockSpec(memory_space=pltpu.VMEM)
    return pl.pallas_call(
        functools.partial(sketch_kernel, sizes, ahead),
        in_specs=[far, far, far],
        out_specs=[far, near, near],
        out_shape=[
            pltpu.HBM((rank, cells), F32),
            jax.ShapeDtypeStruct((2, times, sketch // 2), F32),
            jax.ShapeDtypeStruct((sketch + rank, rank), F32),
        ],
        scratch_shapes=[
            pltpu.VMEM((cells, times), BF16),
            pltpu.VMEM((sketch, cells), BF16),
            pltpu.VMEM((times, rank), BF16),
            pltpu.VMEM((rank, cells), F32),
            pltpu.VMEM((rank, times), BF16),
            pltpu.VMEM((sketch, times), F32),
            pltpu.VMEM((2 * rank, 2 * rank), F32),
            pltpu.VMEM((2 * rank, cells), BF16),
            pltpu.SemaphoreType.DMA((3 * len(sizes) + 1,)),
        ],
        compiler_params=pltpu.CompilerParams(vmem_limit_bytes=44 * 2**20),
        name="sketches",
    )(*[pltpu.with_memory_space_constraint(x, pltpu.HBM) for x in (snapshots, test_rows, range_test)])


def solve_kernel(
    cells_total, owned, crit, mine, range_t, adjoint, species, rates, factors, first, second,
    augmented, lhs, upper, chol
):
    sketch = mine.shape[2] * 2
    rank = crit.shape[1]
    half = sketch // 2
    ends = -(-owned // 8) * 8
    lhs[...] = jnp.zeros_like(lhs)
    for h in range(2):
        lhs[0:owned, h * half : (h + 1) * half] = mine[h]
        for j in range(2):
            for q in range(2):
                place = sketch + j * 4 + h * 2 + q
                lhs[ends + j : ends + j + 1, h * half + q * 64 : h * half + (q + 1) * 64] = crit[
                    place : place + 1, rank // 2 :
                ]
    projected = crit[0:sketch, :]
    turned = projected.T
    augmented[:, 0:rank] = jnp.dot(turned, projected, precision=HIGH, preferred_element_type=F32)
    augmented[:, rank:] = lax.dot_general(turned, lhs[...], NT, precision=HIGH, preferred_element_type=F32)
    gram = crit[sketch:, :]
    row_id = lax.broadcasted_iota(jnp.int32, (rank, rank), 0)
    col_id = lax.broadcasted_iota(jnp.int32, (rank, rank), 1)
    upper[...] = jnp.where(col_id > row_id, gram.T, gram)

    many = ROWS
    sub = lax.broadcasted_iota(jnp.int32, (many, rank), 0)
    lane = lax.broadcasted_iota(jnp.int32, (many, rank), 1)
    tiles = rank // 8
    size = rank // 2
    per = size // many
    for start in range(0, rank, size):
        left, right = [], []
        for i in range(per):
            rows = slice(start + many * i, start + many * (i + 1))
            left.append([augmented[rows, :rank], augmented[rows, rank:]])
            right.append([upper[rows, :]])
        for b in range(per):
            at = start + many * b
            left[b], _ = reduced(left[b], at, sub, False)
            right[b], roots = reduced(right[b], at, sub, True)
            chol[at : at + many, :] = jnp.where(lane >= at + sub, roots, 0.0)
            for i in range(b + 1, b + per):
                left[i % per] = eliminated(left[i % per], at, left[b])
            for i in range(b + 1, per):
                right[i] = eliminated(right[i], at, right[b])
            for i in range(b):
                right[i] = eliminated(right[i], at, right[b])
        panel = [jnp.concatenate([row[p] for row in left], axis=0) for p in range(2)]
        ahead = slice(0 if start + size < rank else rank, 2 * rank)
        panel = jnp.concatenate(panel, axis=1)[:, ahead]
        others = [o for o in (slice(0, start), slice(start + size, rank)) if o.stop > o.start]
        taken = jnp.concatenate([augmented[o, :rank] for o in others], axis=0)
        change = jnp.dot(taken, spread(panel, start, rank), precision=HIGH, preferred_element_type=F32)
        done = 0
        for o in others:
            count = o.stop - o.start
            augmented[o, ahead] = augmented[o, ahead] - change[done : done + count, :]
            done += count
        augmented[start : start + size, ahead] = panel
        rest = slice(start + size, rank)
        if rest.stop > rest.start:
            panel = jnp.concatenate([row[0] for row in right], axis=0)
            upper[rest, :] = upper[rest, :] - jnp.dot(
                upper[rest, :], spread(panel, start, rank), precision=HIGH, preferred_element_type=F32
            )

    solved = augmented[:, rank:]
    out = jnp.dot(chol[...], solved, precision=HIGH, preferred_element_type=F32)
    factors[...] = out[:, 0:owned] * cells_total**-0.5

    rows_here, width = adjoint.shape
    for r in range(rows_here):
        sums = [jnp.zeros((8, width), F32) for _ in range(2)]
        for t in range(tiles):
            part = range_t[8 * t : 8 * t + 8, r * width : (r + 1) * width]
            for j in range(2):
                sums[j] = sums[j] + part * solved[8 * t : 8 * t + 8, ends + j : ends + j + 1]
        for j in range(2):
            (first if j == 1 else second)[r : r + 1, :] = jnp.sum(sums[j], axis=0, keepdims=True)

    kinds = species[...]
    coupling = jnp.zeros(kinds.shape, F32)
    for kind in range(rates.shape[0]):
        coupling = jnp.where(kinds == kind, rates[kind], coupling)
    coupling = STEP_SIZE * coupling
    value = adjoint[...]
    state = first[...]
    none = jnp.zeros((1, width), F32)
    edge = jnp.zeros((rows_here, 1), F32)
    near = jnp.concatenate([none, value[:-1]], axis=0) + jnp.concatenate([value[1:], none], axis=0)
    near = near + jnp.concatenate([edge, value[:, :-1]], axis=1) + jnp.concatenate([value[:, 1:], edge], axis=1)
    first[...] = value + DIFFUSION * (near - 4.0 * value) + coupling * (1.0 - 3.0 * state * state) * value
    state = second[...]
    second[...] = coupling * (1.0 - 3.0 * state * state)


def spread(panel, first, rank):
    rows = [jnp.zeros((first, panel.shape[1]), F32), panel, jnp.zeros((rank - first - panel.shape[0], panel.shape[1]), F32)]
    return jnp.concatenate([r for r in rows if r.shape[0]], axis=0)


def reduced(tile, first_col, sub, want_roots):
    block = tile[0].shape
    cols = [jnp.broadcast_to(tile[0][:, first_col + k : first_col + k + 1], block) for k in range(block[0])]
    roots = tile[0]
    for k in range(block[0]):
        pivot = jnp.broadcast_to(cols[k][k : k + 1, :], block)
        inverse = 1.0 / pivot
        rows = [jnp.broadcast_to(part[k : k + 1, :], block) for part in tile]
        here = sub == k
        if want_roots:
            roots = jnp.where(here, rows[0] * lax.rsqrt(pivot), roots)
        scaled = [row * inverse for row in rows]
        tile = [jnp.where(here, row, part - cols[k] * row) for row, part in zip(scaled, tile)]
        for m in range(k + 1, block[0]):
            value = jnp.broadcast_to(cols[m][k : k + 1, :], block) * inverse
            cols[m] = jnp.where(here, value, cols[m] - cols[k] * value)
    return tile, roots


def eliminated(parts, first_col, tile):
    block = tile[0].shape
    cols = [jnp.broadcast_to(parts[0][:, first_col + k : first_col + k + 1], block) for k in range(block[0])]
    out = []
    for part, known in zip(parts, tile):
        terms = [cols[k] * jnp.broadcast_to(known[k : k + 1, :], block) for k in range(block[0])]
        while len(terms) > 1:
            terms = [terms[i] + terms[i + 1] for i in range(0, len(terms), 2)]
        out.append(part - terms[0])
    return out


def fetch_kernel(source, out, sems):
    pieces = sems.shape[0]
    many = source.shape[0] // pieces
    copies = [
        pltpu.make_async_copy(source.at[pl.ds(i * many, many)], out.at[pl.ds(i * many, many)], sems.at[i])
        for i in range(pieces)
    ]
    for copy in copies:
        copy.start()
    for copy in copies:
        copy.wait()


def fetch(array):
    return pl.pallas_call(
        fetch_kernel,
        in_specs=[pl.BlockSpec(memory_space=pltpu.HBM)],
        out_specs=pl.BlockSpec(memory_space=pltpu.VMEM),
        out_shape=jax.ShapeDtypeStruct(array.shape, array.dtype),
        scratch_shapes=[pltpu.SemaphoreType.DMA((8,))],
        compiler_params=pltpu.CompilerParams(vmem_limit_bytes=2**20),
        cost_estimate=pl.CostEstimate(flops=0, bytes_accessed=8 * array.size, transcendentals=0),
        name="fetch",
    )(pltpu.with_memory_space_constraint(array, pltpu.HBM))


def solve(crit, mine, range_t, adjoint, species, rates, cells_total):
    owned = mine.shape[1]
    rank = crit.shape[1]
    sketch = 2 * mine.shape[2]
    vmem = pl.BlockSpec(memory_space=pltpu.VMEM)
    return pl.pallas_call(
        functools.partial(solve_kernel, cells_total, owned),
        in_specs=[vmem, vmem, vmem, vmem, vmem, pl.BlockSpec(memory_space=pltpu.SMEM)],
        out_specs=[vmem, vmem, vmem],
        out_shape=[
            jax.ShapeDtypeStruct((rank, owned), F32),
            jax.ShapeDtypeStruct(adjoint.shape, F32),
            jax.ShapeDtypeStruct(adjoint.shape, F32),
        ],
        scratch_shapes=[
            pltpu.VMEM((rank, 2 * rank), F32),
            pltpu.VMEM((rank, sketch), F32),
            pltpu.VMEM((rank, rank), F32),
            pltpu.VMEM((rank, rank), F32),
        ],
        compiler_params=pltpu.CompilerParams(vmem_limit_bytes=16 * 2**20),
        name="solve",
    )(crit, mine, range_t, adjoint, species, rates)


def partners(count, shift, other):
    return [(i, i ^ (other << shift)) for i in range(count)]


def member(shift, size):
    return (lax.axis_index(AXES) >> shift) & (size - 1)


def pick(pieces, index):
    return lax.dynamic_index_in_dim(pieces, index, 0, keepdims=False)


def summed_pieces(pieces, count, shift):
    size = pieces.shape[0]
    me = member(shift, size)
    got = [lax.ppermute(pick(pieces, me ^ p), AXES, partners(count, shift, p)) for p in range(size - 1, 0, -1)]
    total = pick(pieces, me)
    for piece in got:
        total = total + piece
    return total


def gathered_pieces(piece, count, shift, size):
    me = member(shift, size)
    got = [lax.ppermute(piece, AXES, partners(count, shift, p)) for p in range(size - 1, 0, -1)]
    out = jnp.zeros((size,) + piece.shape, piece.dtype)
    for p, part in zip([0] + list(range(size - 1, 0, -1)), [piece] + got):
        out = lax.dynamic_update_index_in_dim(out, part, me ^ p, 0)
    return out


def stages(count):
    bits = count.bit_length() - 1
    out, shift = [(0, 2)], 1
    while shift < bits:
        width = min(2, bits - shift)
        out.append((shift, 1 << width))
        shift += width
    return out


def reduce_sketches(crit, ct, range_t, count):
    plan = stages(count)
    halves, times, width = ct.shape
    owned = times // count
    left = count
    for shift, size in plan[:-1]:
        left //= size
        crit = crit.reshape(size, -1, width)
        ct = ct.reshape(halves, left, size, owned, width)
        ct = jnp.moveaxis(ct, 2, 0).reshape(size, -1, width)
        split = crit.shape[1]
        both = summed_pieces(jnp.concatenate([crit, ct], axis=1), count, shift)
        crit, ct = both[:split], both[split:].reshape(halves, left * owned, width)
    shift, size = plan[-1]
    crit, ct, range_t = lax.optimization_barrier((crit, ct, range_t))
    range_t = fetch(range_t)
    ct = ct.reshape(halves, size, owned, width)
    ct = jnp.moveaxis(ct, 1, 0).reshape(size, -1, width)
    split = crit.shape[0]
    whole = jnp.broadcast_to(crit[None], (size,) + crit.shape)
    both = summed_pieces(jnp.concatenate([whole, ct], axis=1), count, shift)
    crit, mine = both[:split], both[split:].reshape(halves, owned, width)
    for shift, size in plan[-2::-1]:
        crit = gathered_pieces(crit, count, shift, size).reshape(-1, width)
    return crit, mine, range_t


def shards(snapshots, range_test, test_rows, species, reaction_rates, adjoint_end):
    count = lax.axis_size(AXES)
    cells_total = snapshots.shape[0] * count
    range_t, ct, crit = sketches(snapshots, range_test, test_rows)
    crit, mine, range_t = reduce_sketches(crit, ct, range_t, count)
    time_factors, partial, rate = solve(crit, mine, range_t, adjoint_end, species, reaction_rates, cells_total)
    device = lax.axis_index(AXES)
    even = device % 2 == 0
    head = jnp.concatenate([partial[:1], adjoint_end[:1]], axis=0)
    tail = jnp.concatenate([partial[-1:], adjoint_end[-1:]], axis=0)
    pairs = [(i, i ^ 1) for i in range(count)]
    across = [(i, i + 1) for i in range(1, count - 1, 2)] + [(i + 1, i) for i in range(1, count - 1, 2)]
    far = lax.ppermute(jnp.where(even, head, tail), AXES, across)
    near = lax.ppermute(jnp.where(even, tail, head), AXES, pairs)
    above = jnp.where(even, far, near)
    below = jnp.where(even, near, far)
    adjoint = jnp.concatenate(
        [partial[:1] + DIFFUSION * above[1:], partial[1:-1], partial[-1:] + DIFFUSION * below[1:]], axis=0
    )
    top = jnp.where(device > 0, above[:1] + DIFFUSION * adjoint_end[:1], 0.0)
    bottom = jnp.where(device < count - 1, below[:1] + DIFFUSION * adjoint_end[-1:], 0.0)
    padded = jnp.concatenate([top, adjoint, bottom], axis=0)
    sideways = jnp.pad(adjoint, ((0, 0), (1, 1)))
    laplace = padded[2:] + padded[:-2] + sideways[:, 2:] + sideways[:, :-2] - 4.0 * adjoint
    return (adjoint + DIFFUSION * laplace + rate * adjoint, time_factors)


def solution(mesh):
    return jax.shard_map(
        shards,
        mesh=mesh,
        in_specs=(P(AXES, None), P(), P(None, AXES), P(AXES, None), P(), P(AXES, None)),
        out_specs=(P(AXES, None), P(None, AXES)),
        check_vma=False,
    )
```

```python
import functools

import jax
import jax.numpy as jnp
from jax import lax
from jax.experimental import pallas as pl
from jax.experimental.pallas import tpu as pltpu
from jax.sharding import PartitionSpec as P

DIFFUSION = 0.2
STEP_SIZE = 0.05
AXES = ("space", "tm")
ROWS = 16
HIGH = lax.Precision.HIGHEST
NT = (((1,), (1,)), ((), ()))
F32 = jnp.float32
BF16 = jnp.bfloat16


def sketch_kernel(
    sizes, ahead, snap, test, om, range_out, ct, crit,
    snap_v, test_v, om_v, range_t, om_t, corange, gram, split, sems,
):
    times = snap.shape[1]
    rank = om.shape[1]
    sketch = test.shape[0]
    blocks = len(sizes)
    places = [pl.ds(sum(sizes[:i]), sizes[i]) for i in range(blocks)]

    def copies(i):
        at = places[i]
        return (
            pltpu.make_async_copy(snap.at[at, :], snap_v.at[at, :], sems.at[2 * i]),
            pltpu.make_async_copy(test.at[:, at], test_v.at[:, at], sems.at[2 * i + 1]),
        )

    def leaving(i):
        return pltpu.make_async_copy(range_t.at[:, places[i]], range_out.at[:, places[i]], sems.at[2 * blocks + 1 + i])

    def gram_of(i):
        part = split[:, places[i]]
        return lax.dot_general(part, part[0:rank], NT, preferred_element_type=F32)

    own = pltpu.make_async_copy(om, om_v, sems.at[2 * blocks])
    own.start()
    for i in range(min(ahead, blocks)):
        for copy in copies(i):
            copy.start()
    corange[...] = jnp.zeros_like(corange)
    gram[...] = jnp.zeros_like(gram)
    own.wait()
    om_t[...] = om_v[...].astype(F32).T.astype(BF16)
    for i in range(blocks):
        for copy in copies(i):
            copy.wait()
        if i + ahead < blocks:
            for copy in copies(i + ahead):
                copy.start()
        at = places[i]
        states = snap_v[at, :]
        if i:
            gram[...] += gram_of(i - 1)
        rt = lax.dot_general(om_t[...], states, NT, preferred_element_type=F32)
        range_t[:, at] = rt
        leaving(i).start()
        upper = rt.astype(BF16)
        split[0:rank, at] = upper
        split[rank:, at] = (rt - upper.astype(F32)).astype(BF16)
        corange[...] += jnp.dot(test_v[:, at], states, preferred_element_type=F32)
    gram[...] += gram_of(blocks - 1)
    whole = corange[...]
    high = whole.astype(BF16)
    rest = whole - high.astype(F32)
    middle = rest.astype(BF16)
    low = (rest - middle.astype(F32)).astype(BF16)
    projected = jnp.zeros((sketch, rank), F32)
    for part in (low, middle, high):
        projected = projected + jnp.dot(part, om_v[...], preferred_element_type=F32)
    crit[0:sketch, :] = projected
    cross = gram[rank:, :]
    crit[sketch:, :] = gram[0:rank, :] + cross + cross.T
    half = sketch // 2
    for h in range(2):
        turned = whole[h * half : (h + 1) * half, :].T
        ct[h] = turned
        for j in range(2):
            row = turned[times - 2 + j : times - 1 + j, :]
            for q in range(2):
                there = sketch + j * 4 + h * 2 + q
                crit[there : there + 1, rank // 2 :] = row[:, q * 64 : (q + 1) * 64]
    for i in range(blocks):
        leaving(i).wait()


def sketches(snapshots, range_test, test_rows, shares=(1, 1, 2, 2, 2), ahead=5):
    cells, times = snapshots.shape
    rank = range_test.shape[1]
    sketch = test_rows.shape[0]
    sizes = [share * cells // sum(shares) for share in shares]
    far = pl.BlockSpec(memory_space=pltpu.HBM)
    near = pl.BlockSpec(memory_space=pltpu.VMEM)
    return pl.pallas_call(
        functools.partial(sketch_kernel, sizes, ahead),
        in_specs=[far, far, far],
        out_specs=[far, near, near],
        out_shape=[
            pltpu.HBM((rank, cells), F32),
            jax.ShapeDtypeStruct((2, times, sketch // 2), F32),
            jax.ShapeDtypeStruct((sketch + rank, rank), F32),
        ],
        scratch_shapes=[
            pltpu.VMEM((cells, times), BF16),
            pltpu.VMEM((sketch, cells), BF16),
            pltpu.VMEM((times, rank), BF16),
            pltpu.VMEM((rank, cells), F32),
            pltpu.VMEM((rank, times), BF16),
            pltpu.VMEM((sketch, times), F32),
            pltpu.VMEM((2 * rank, rank), F32),
            pltpu.VMEM((2 * rank, cells), BF16),
            pltpu.SemaphoreType.DMA((3 * len(sizes) + 1,)),
        ],
        compiler_params=pltpu.CompilerParams(vmem_limit_bytes=44 * 2**20),
        name="sketches",
    )(*[pltpu.with_memory_space_constraint(x, pltpu.HBM) for x in (snapshots, test_rows, range_test)])


def solve_kernel(
    cells_total, owned, crit, mine, range_t, adjoint, species, rates, factors, first, second,
    augmented, lhs, upper, chol
):
    sketch = mine.shape[2] * 2
    rank = crit.shape[1]
    half = sketch // 2
    ends = -(-owned // 8) * 8
    lhs[...] = jnp.zeros_like(lhs)
    for h in range(2):
        lhs[0:owned, h * half : (h + 1) * half] = mine[h]
        for j in range(2):
            for q in range(2):
                place = sketch + j * 4 + h * 2 + q
                lhs[ends + j : ends + j + 1, h * half + q * 64 : h * half + (q + 1) * 64] = crit[
                    place : place + 1, rank // 2 :
                ]
    projected = crit[0:sketch, :]
    turned = projected.T
    augmented[:, 0:rank] = jnp.dot(turned, projected, precision=HIGH, preferred_element_type=F32)
    augmented[:, rank:] = lax.dot_general(turned, lhs[...], NT, precision=HIGH, preferred_element_type=F32)
    gram = crit[sketch:, :]
    row_id = lax.broadcasted_iota(jnp.int32, (rank, rank), 0)
    col_id = lax.broadcasted_iota(jnp.int32, (rank, rank), 1)
    upper[...] = jnp.where(col_id > row_id, gram.T, gram)

    many = ROWS
    sub = lax.broadcasted_iota(jnp.int32, (many, rank), 0)
    lane = lax.broadcasted_iota(jnp.int32, (many, rank), 1)
    tiles = rank // 8
    size = rank // 2
    per = size // many
    for start in range(0, rank, size):
        left, right = [], []
        for i in range(per):
            rows = slice(start + many * i, start + many * (i + 1))
            left.append([augmented[rows, :rank], augmented[rows, rank:]])
            right.append([upper[rows, :]])
        for b in range(per):
            at = start + many * b
            left[b], _ = reduced(left[b], at, sub, False)
            right[b], roots = reduced(right[b], at, sub, True)
            chol[at : at + many, :] = jnp.where(lane >= at + sub, roots, 0.0)
            for i in range(b + 1, b + per):
                left[i % per] = eliminated(left[i % per], at, left[b])
            for i in range(b + 1, per):
                right[i] = eliminated(right[i], at, right[b])
            for i in range(b):
                right[i] = eliminated(right[i], at, right[b])
        panel = [jnp.concatenate([row[p] for row in left], axis=0) for p in range(2)]
        ahead = slice(0 if start + size < rank else rank, 2 * rank)
        panel = jnp.concatenate(panel, axis=1)[:, ahead]
        others = [o for o in (slice(0, start), slice(start + size, rank)) if o.stop > o.start]
        taken = jnp.concatenate([augmented[o, :rank] for o in others], axis=0)
        change = jnp.dot(taken, spread(panel, start, rank), precision=HIGH, preferred_element_type=F32)
        done = 0
        for o in others:
            count = o.stop - o.start
            augmented[o, ahead] = augmented[o, ahead] - change[done : done + count, :]
            done += count
        augmented[start : start + size, ahead] = panel
        rest = slice(start + size, rank)
        if rest.stop > rest.start:
            panel = jnp.concatenate([row[0] for row in right], axis=0)
            upper[rest, :] = upper[rest, :] - jnp.dot(
                upper[rest, :], spread(panel, start, rank), precision=HIGH, preferred_element_type=F32
            )

    solved = augmented[:, rank:]
    out = jnp.dot(chol[...], solved, precision=HIGH, preferred_element_type=F32)
    factors[...] = out[:, 0:owned] * cells_total**-0.5

    rows_here, width = adjoint.shape
    for r in range(rows_here):
        sums = [jnp.zeros((8, width), F32) for _ in range(2)]
        for t in range(tiles):
            part = range_t[8 * t : 8 * t + 8, r * width : (r + 1) * width]
            for j in range(2):
                sums[j] = sums[j] + part * solved[8 * t : 8 * t + 8, ends + j : ends + j + 1]
        for j in range(2):
            (first if j == 1 else second)[r : r + 1, :] = jnp.sum(sums[j], axis=0, keepdims=True)

    kinds = species[...]
    coupling = jnp.zeros(kinds.shape, F32)
    for kind in range(rates.shape[0]):
        coupling = jnp.where(kinds == kind, rates[kind], coupling)
    coupling = STEP_SIZE * coupling
    value = adjoint[...]
    state = first[...]
    none = jnp.zeros((1, width), F32)
    edge = jnp.zeros((rows_here, 1), F32)
    near = jnp.concatenate([none, value[:-1]], axis=0) + jnp.concatenate([value[1:], none], axis=0)
    near = near + jnp.concatenate([edge, value[:, :-1]], axis=1) + jnp.concatenate([value[:, 1:], edge], axis=1)
    first[...] = value + DIFFUSION * (near - 4.0 * value) + coupling * (1.0 - 3.0 * state * state) * value
    state = second[...]
    second[...] = coupling * (1.0 - 3.0 * state * state)


def spread(panel, first, rank):
    rows = [jnp.zeros((first, panel.shape[1]), F32), panel, jnp.zeros((rank - first - panel.shape[0], panel.shape[1]), F32)]
    return jnp.concatenate([r for r in rows if r.shape[0]], axis=0)


def reduced(tile, first_col, sub, want_roots):
    block = tile[0].shape
    cols = [jnp.broadcast_to(tile[0][:, first_col + k : first_col + k + 1], block) for k in range(block[0])]
    roots = tile[0]
    for k in range(block[0]):
        pivot = jnp.broadcast_to(cols[k][k : k + 1, :], block)
        inverse = 1.0 / pivot
        rows = [jnp.broadcast_to(part[k : k + 1, :], block) for part in tile]
        here = sub == k
        if want_roots:
            roots = jnp.where(here, rows[0] * lax.rsqrt(pivot), roots)
        scaled = [row * inverse for row in rows]
        tile = [jnp.where(here, row, part - cols[k] * row) for row, part in zip(scaled, tile)]
        for m in range(k + 1, block[0]):
            value = jnp.broadcast_to(cols[m][k : k + 1, :], block) * inverse
            cols[m] = jnp.where(here, value, cols[m] - cols[k] * value)
    return tile, roots


def eliminated(parts, first_col, tile):
    block = tile[0].shape
    cols = [jnp.broadcast_to(parts[0][:, first_col + k : first_col + k + 1], block) for k in range(block[0])]
    out = []
    for part, known in zip(parts, tile):
        terms = [cols[k] * jnp.broadcast_to(known[k : k + 1, :], block) for k in range(block[0])]
        while len(terms) > 1:
            terms = [terms[i] + terms[i + 1] for i in range(0, len(terms), 2)]
        out.append(part - terms[0])
    return out


def fetch_kernel(source, out, sems):
    pieces = sems.shape[0]
    many = source.shape[0] // pieces
    copies = [
        pltpu.make_async_copy(source.at[pl.ds(i * many, many)], out.at[pl.ds(i * many, many)], sems.at[i])
        for i in range(pieces)
    ]
    for copy in copies:
        copy.start()
    for copy in copies:
        copy.wait()


def fetch(array):
    return pl.pallas_call(
        fetch_kernel,
        in_specs=[pl.BlockSpec(memory_space=pltpu.HBM)],
        out_specs=pl.BlockSpec(memory_space=pltpu.VMEM),
        out_shape=jax.ShapeDtypeStruct(array.shape, array.dtype),
        scratch_shapes=[pltpu.SemaphoreType.DMA((8,))],
        compiler_params=pltpu.CompilerParams(vmem_limit_bytes=2**20),
        cost_estimate=pl.CostEstimate(flops=0, bytes_accessed=8 * array.size, transcendentals=0),
        name="fetch",
    )(pltpu.with_memory_space_constraint(array, pltpu.HBM))


def solve(crit, mine, range_t, adjoint, species, rates, cells_total):
    owned = mine.shape[1]
    rank = crit.shape[1]
    sketch = 2 * mine.shape[2]
    vmem = pl.BlockSpec(memory_space=pltpu.VMEM)
    return pl.pallas_call(
        functools.partial(solve_kernel, cells_total, owned),
        in_specs=[vmem, vmem, vmem, vmem, vmem, pl.BlockSpec(memory_space=pltpu.SMEM)],
        out_specs=[vmem, vmem, vmem],
        out_shape=[
            jax.ShapeDtypeStruct((rank, owned), F32),
            jax.ShapeDtypeStruct(adjoint.shape, F32),
            jax.ShapeDtypeStruct(adjoint.shape, F32),
        ],
        scratch_shapes=[
            pltpu.VMEM((rank, 2 * rank), F32),
            pltpu.VMEM((rank, sketch), F32),
            pltpu.VMEM((rank, rank), F32),
            pltpu.VMEM((rank, rank), F32),
        ],
        compiler_params=pltpu.CompilerParams(vmem_limit_bytes=16 * 2**20),
        name="solve",
    )(crit, mine, range_t, adjoint, species, rates)


def partners(count, shift, other):
    return [(i, i ^ (other << shift)) for i in range(count)]


def member(shift, size):
    return (lax.axis_index(AXES) >> shift) & (size - 1)


def pick(pieces, index):
    return lax.dynamic_index_in_dim(pieces, index, 0, keepdims=False)


def summed_pieces(pieces, count, shift):
    size = pieces.shape[0]
    me = member(shift, size)
    got = [lax.ppermute(pick(pieces, me ^ p), AXES, partners(count, shift, p)) for p in range(size - 1, 0, -1)]
    total = pick(pieces, me)
    for piece in got:
        total = total + piece
    return total


def gathered_pieces(piece, count, shift, size):
    me = member(shift, size)
    got = [lax.ppermute(piece, AXES, partners(count, shift, p)) for p in range(size - 1, 0, -1)]
    out = jnp.zeros((size,) + piece.shape, piece.dtype)
    for p, part in zip([0] + list(range(size - 1, 0, -1)), [piece] + got):
        out = lax.dynamic_update_index_in_dim(out, part, me ^ p, 0)
    return out


def stages(count):
    bits = count.bit_length() - 1
    out, shift = [(0, 2)], 1
    while shift < bits:
        width = min(2, bits - shift)
        out.append((shift, 1 << width))
        shift += width
    return out


def reduce_sketches(crit, ct, range_t, count):
    plan = stages(count)
    halves, times, width = ct.shape
    owned = times // count
    left = count
    for shift, size in plan[:-1]:
        left //= size
        crit = crit.reshape(size, -1, width)
        ct = ct.reshape(halves, left, size, owned, width)
        ct = jnp.moveaxis(ct, 2, 0).reshape(size, -1, width)
        split = crit.shape[1]
        both = summed_pieces(jnp.concatenate([crit, ct], axis=1), count, shift)
        crit, ct = both[:split], both[split:].reshape(halves, left * owned, width)
    shift, size = plan[-1]
    crit, ct, range_t = lax.optimization_barrier((crit, ct, range_t))
    range_t = fetch(range_t)
    ct = ct.reshape(halves, size, owned, width)
    ct = jnp.moveaxis(ct, 1, 0).reshape(size, -1, width)
    split = crit.shape[0]
    whole = jnp.broadcast_to(crit[None], (size,) + crit.shape)
    both = summed_pieces(jnp.concatenate([whole, ct], axis=1), count, shift)
    crit, mine = both[:split], both[split:].reshape(halves, owned, width)
    for shift, size in plan[-2::-1]:
        crit = gathered_pieces(crit, count, shift, size).reshape(-1, width)
    return crit, mine, range_t


def shards(snapshots, range_test, test_rows, species, reaction_rates, adjoint_end):
    count = lax.axis_size(AXES)
    cells_total = snapshots.shape[0] * count
    range_t, ct, crit = sketches(snapshots, range_test, test_rows)
    crit, mine, range_t = reduce_sketches(crit, ct, range_t, count)
    time_factors, partial, rate = solve(crit, mine, range_t, adjoint_end, species, reaction_rates, cells_total)
    device = lax.axis_index(AXES)
    even = device % 2 == 0
    head = jnp.concatenate([partial[:1], adjoint_end[:1]], axis=0)
    tail = jnp.concatenate([partial[-1:], adjoint_end[-1:]], axis=0)
    pairs = [(i, i ^ 1) for i in range(count)]
    across = [(i, i + 1) for i in range(1, count - 1, 2)] + [(i + 1, i) for i in range(1, count - 1, 2)]
    far = lax.ppermute(jnp.where(even, head, tail), AXES, across)
    near = lax.ppermute(jnp.where(even, tail, head), AXES, pairs)
    above = jnp.where(even, far, near)
    below = jnp.where(even, near, far)
    adjoint = jnp.concatenate(
        [partial[:1] + DIFFUSION * above[1:], partial[1:-1], partial[-1:] + DIFFUSION * below[1:]], axis=0
    )
    top = jnp.where(device > 0, above[:1] + DIFFUSION * adjoint_end[:1], 0.0)
    bottom = jnp.where(device < count - 1, below[:1] + DIFFUSION * adjoint_end[-1:], 0.0)
    padded = jnp.concatenate([top, adjoint, bottom], axis=0)
    sideways = jnp.pad(adjoint, ((0, 0), (1, 1)))
    laplace = padded[2:] + padded[:-2] + sideways[:, 2:] + sideways[:, :-2] - 4.0 * adjoint
    return (adjoint + DIFFUSION * laplace + rate * adjoint, time_factors)


def solution(mesh):
    return jax.shard_map(
        shards,
        mesh=mesh,
        in_specs=(P(AXES, None), P(), P(None, AXES), P(AXES, None), P(), P(AXES, None)),
        out_specs=(P(AXES, None), P(None, AXES)),
        check_vma=False,
    )
```

```python
import functools

import jax
import jax.numpy as jnp
from jax import lax
from jax.experimental import pallas as pl
from jax.experimental.pallas import tpu as pltpu
from jax.sharding import PartitionSpec as P

DIFFUSION = 0.2
STEP_SIZE = 0.05
AXES = ("space", "tm")
ROWS = 16
HIGH = lax.Precision.HIGHEST
NT = (((1,), (1,)), ((), ()))
F32 = jnp.float32
BF16 = jnp.bfloat16


def sketch_kernel(
    sizes, ahead, snap, test, om, range_out, ct, crit,
    snap_v, test_v, om_v, range_t, om_t, corange, gram, split, sems,
):
    times = snap.shape[1]
    rank = om.shape[1]
    sketch = test.shape[0]
    blocks = len(sizes)
    places = [pl.ds(sum(sizes[:i]), sizes[i]) for i in range(blocks)]

    def copies(i):
        at = places[i]
        return (
            pltpu.make_async_copy(snap.at[at, :], snap_v.at[at, :], sems.at[2 * i]),
            pltpu.make_async_copy(test.at[:, at], test_v.at[:, at], sems.at[2 * i + 1]),
        )

    def leaving(i):
        return pltpu.make_async_copy(range_t.at[:, places[i]], range_out.at[:, places[i]], sems.at[2 * blocks + 1 + i])

    def gram_of(i):
        part = split[:, places[i]]
        return lax.dot_general(part, part[0:rank], NT, preferred_element_type=F32)

    own = pltpu.make_async_copy(om, om_v, sems.at[2 * blocks])
    own.start()
    for i in range(min(ahead, blocks)):
        for copy in copies(i):
            copy.start()
    corange[...] = jnp.zeros_like(corange)
    gram[...] = jnp.zeros_like(gram)
    own.wait()
    om_t[...] = om_v[...].astype(F32).T.astype(BF16)
    for i in range(blocks):
        for copy in copies(i):
            copy.wait()
        if i + ahead < blocks:
            for copy in copies(i + ahead):
                copy.start()
        at = places[i]
        states = snap_v[at, :]
        if i:
            gram[...] += gram_of(i - 1)
        rt = lax.dot_general(om_t[...], states, NT, preferred_element_type=F32)
        range_t[:, at] = rt
        leaving(i).start()
        upper = rt.astype(BF16)
        split[0:rank, at] = upper
        split[rank:, at] = (rt - upper.astype(F32)).astype(BF16)
        corange[...] += jnp.dot(test_v[:, at], states, preferred_element_type=F32)
    gram[...] += gram_of(blocks - 1)
    whole = corange[...]
    high = whole.astype(BF16)
    rest = whole - high.astype(F32)
    middle = rest.astype(BF16)
    low = (rest - middle.astype(F32)).astype(BF16)
    projected = jnp.zeros((sketch, rank), F32)
    for part in (low, middle, high):
        projected = projected + jnp.dot(part, om_v[...], preferred_element_type=F32)
    crit[0:sketch, :] = projected
    cross = gram[rank:, :]
    crit[sketch:, :] = gram[0:rank, :] + cross + cross.T
    half = sketch // 2
    for h in range(2):
        turned = whole[h * half : (h + 1) * half, :].T
        ct[h] = turned
        for j in range(2):
            row = turned[times - 2 + j : times - 1 + j, :]
            for q in range(2):
                there = sketch + j * 4 + h * 2 + q
                crit[there : there + 1, rank // 2 :] = row[:, q * 64 : (q + 1) * 64]
    for i in range(blocks):
        leaving(i).wait()


def sketches(snapshots, range_test, test_rows, shares=(1, 1, 2, 2, 2), ahead=5):
    cells, times = snapshots.shape
    rank = range_test.shape[1]
    sketch = test_rows.shape[0]
    sizes = [share * cells // sum(shares) for share in shares]
    far = pl.BlockSpec(memory_space=pltpu.HBM)
    near = pl.BlockSpec(memory_space=pltpu.VMEM)
    return pl.pallas_call(
        functools.partial(sketch_kernel, sizes, ahead),
        in_specs=[far, far, far],
        out_specs=[far, near, near],
        out_shape=[
            pltpu.HBM((rank, cells), F32),
            jax.ShapeDtypeStruct((2, times, sketch // 2), F32),
            jax.ShapeDtypeStruct((sketch + rank, rank), F32),
        ],
        scratch_shapes=[
            pltpu.VMEM((cells, times), BF16),
            pltpu.VMEM((sketch, cells), BF16),
            pltpu.VMEM((times, rank), BF16),
            pltpu.VMEM((rank, cells), F32),
            pltpu.VMEM((rank, times), BF16),
            pltpu.VMEM((sketch, times), F32),
            pltpu.VMEM((2 * rank, rank), F32),
            pltpu.VMEM((2 * rank, cells), BF16),
            pltpu.SemaphoreType.DMA((3 * len(sizes) + 1,)),
        ],
        compiler_params=pltpu.CompilerParams(vmem_limit_bytes=44 * 2**20),
        name="sketches",
    )(*[pltpu.with_memory_space_constraint(x, pltpu.HBM) for x in (snapshots, test_rows, range_test)])


def solve_kernel(
    cells_total, owned, crit, mine, range_t, adjoint, species, rates, factors, first, second,
    augmented, lhs, upper, chol
):
    sketch = mine.shape[2] * 2
    rank = crit.shape[1]
    half = sketch // 2
    ends = -(-owned // 8) * 8
    lhs[...] = jnp.zeros_like(lhs)
    for h in range(2):
        lhs[0:owned, h * half : (h + 1) * half] = mine[h]
        for j in range(2):
            for q in range(2):
                place = sketch + j * 4 + h * 2 + q
                lhs[ends + j : ends + j + 1, h * half + q * 64 : h * half + (q + 1) * 64] = crit[
                    place : place + 1, rank // 2 :
                ]
    projected = crit[0:sketch, :]
    turned = projected.T
    augmented[:, 0:rank] = jnp.dot(turned, projected, precision=HIGH, preferred_element_type=F32)
    augmented[:, rank:] = lax.dot_general(turned, lhs[...], NT, precision=HIGH, preferred_element_type=F32)
    gram = crit[sketch:, :]
    row_id = lax.broadcasted_iota(jnp.int32, (rank, rank), 0)
    col_id = lax.broadcasted_iota(jnp.int32, (rank, rank), 1)
    upper[...] = jnp.where(col_id > row_id, gram.T, gram)

    many = ROWS
    sub = lax.broadcasted_iota(jnp.int32, (many, rank), 0)
    lane = lax.broadcasted_iota(jnp.int32, (many, rank), 1)
    tiles = rank // 8
    size = rank // 2
    per = size // many
    for start in range(0, rank, size):
        left, right = [], []
        for i in range(per):
            rows = slice(start + many * i, start + many * (i + 1))
            left.append([augmented[rows, :rank], augmented[rows, rank:]])
            right.append([upper[rows, :]])
        for b in range(per):
            at = start + many * b
            left[b], _ = reduced(left[b], at, sub, False)
            right[b], roots = reduced(right[b], at, sub, True)
            chol[at : at + many, :] = jnp.where(lane >= at + sub, roots, 0.0)
            for i in range(b + 1, b + per):
                left[i % per] = eliminated(left[i % per], at, left[b])
            for i in range(b + 1, per):
                right[i] = eliminated(right[i], at, right[b])
            for i in range(b):
                right[i] = eliminated(right[i], at, right[b])
        panel = [jnp.concatenate([row[p] for row in left], axis=0) for p in range(2)]
        ahead = slice(0 if start + size < rank else rank, 2 * rank)
        panel = jnp.concatenate(panel, axis=1)[:, ahead]
        others = [o for o in (slice(0, start), slice(start + size, rank)) if o.stop > o.start]
        taken = jnp.concatenate([augmented[o, :rank] for o in others], axis=0)
        change = jnp.dot(taken, spread(panel, start, rank), precision=HIGH, preferred_element_type=F32)
        done = 0
        for o in others:
            count = o.stop - o.start
            augmented[o, ahead] = augmented[o, ahead] - change[done : done + count, :]
            done += count
        augmented[start : start + size, ahead] = panel
        rest = slice(start + size, rank)
        if rest.stop > rest.start:
            panel = jnp.concatenate([row[0] for row in right], axis=0)
            upper[rest, :] = upper[rest, :] - jnp.dot(
                upper[rest, :], spread(panel, start, rank), precision=HIGH, preferred_element_type=F32
            )

    solved = augmented[:, rank:]
    out = jnp.dot(chol[...], solved, precision=HIGH, preferred_element_type=F32)
    factors[...] = out[:, 0:owned] * cells_total**-0.5

    rows_here, width = adjoint.shape
    for r in range(rows_here):
        sums = [jnp.zeros((8, width), F32) for _ in range(2)]
        for t in range(tiles):
            part = range_t[8 * t : 8 * t + 8, r * width : (r + 1) * width]
            for j in range(2):
                sums[j] = sums[j] + part * solved[8 * t : 8 * t + 8, ends + j : ends + j + 1]
        for j in range(2):
            (first if j == 1 else second)[r : r + 1, :] = jnp.sum(sums[j], axis=0, keepdims=True)

    kinds = species[...]
    coupling = jnp.zeros(kinds.shape, F32)
    for kind in range(rates.shape[0]):
        coupling = jnp.where(kinds == kind, rates[kind], coupling)
    coupling = STEP_SIZE * coupling
    value = adjoint[...]
    state = first[...]
    none = jnp.zeros((1, width), F32)
    edge = jnp.zeros((rows_here, 1), F32)
    near = jnp.concatenate([none, value[:-1]], axis=0) + jnp.concatenate([value[1:], none], axis=0)
    near = near + jnp.concatenate([edge, value[:, :-1]], axis=1) + jnp.concatenate([value[:, 1:], edge], axis=1)
    first[...] = value + DIFFUSION * (near - 4.0 * value) + coupling * (1.0 - 3.0 * state * state) * value
    state = second[...]
    second[...] = coupling * (1.0 - 3.0 * state * state)


def spread(panel, first, rank):
    rows = [jnp.zeros((first, panel.shape[1]), F32), panel, jnp.zeros((rank - first - panel.shape[0], panel.shape[1]), F32)]
    return jnp.concatenate([r for r in rows if r.shape[0]], axis=0)


def reduced(tile, first_col, sub, want_roots):
    block = tile[0].shape
    cols = [jnp.broadcast_to(tile[0][:, first_col + k : first_col + k + 1], block) for k in range(block[0])]
    roots = tile[0]
    for k in range(block[0]):
        pivot = jnp.broadcast_to(cols[k][k : k + 1, :], block)
        inverse = 1.0 / pivot
        rows = [jnp.broadcast_to(part[k : k + 1, :], block) for part in tile]
        here = sub == k
        if want_roots:
            roots = jnp.where(here, rows[0] * lax.rsqrt(pivot), roots)
        scaled = [row * inverse for row in rows]
        tile = [jnp.where(here, row, part - cols[k] * row) for row, part in zip(scaled, tile)]
        for m in range(k + 1, block[0]):
            value = jnp.broadcast_to(cols[m][k : k + 1, :], block) * inverse
            cols[m] = jnp.where(here, value, cols[m] - cols[k] * value)
    return tile, roots


def eliminated(parts, first_col, tile):
    block = tile[0].shape
    cols = [jnp.broadcast_to(parts[0][:, first_col + k : first_col + k + 1], block) for k in range(block[0])]
    out = []
    for part, known in zip(parts, tile):
        terms = [cols[k] * jnp.broadcast_to(known[k : k + 1, :], block) for k in range(block[0])]
        while len(terms) > 1:
            terms = [terms[i] + terms[i + 1] for i in range(0, len(terms), 2)]
        out.append(part - terms[0])
    return out


def fetch_kernel(source, out, sems):
    pieces = sems.shape[0]
    many = source.shape[0] // pieces
    copies = [
        pltpu.make_async_copy(source.at[pl.ds(i * many, many)], out.at[pl.ds(i * many, many)], sems.at[i])
        for i in range(pieces)
    ]
    for copy in copies:
        copy.start()
    for copy in copies:
        copy.wait()


def fetch(array):
    return pl.pallas_call(
        fetch_kernel,
        in_specs=[pl.BlockSpec(memory_space=pltpu.HBM)],
        out_specs=pl.BlockSpec(memory_space=pltpu.VMEM),
        out_shape=jax.ShapeDtypeStruct(array.shape, array.dtype),
        scratch_shapes=[pltpu.SemaphoreType.DMA((8,))],
        compiler_params=pltpu.CompilerParams(vmem_limit_bytes=2**20),
        cost_estimate=pl.CostEstimate(flops=0, bytes_accessed=8 * array.size, transcendentals=0),
        name="fetch",
    )(pltpu.with_memory_space_constraint(array, pltpu.HBM))


def solve(crit, mine, range_t, adjoint, species, rates, cells_total):
    owned = mine.shape[1]
    rank = crit.shape[1]
    sketch = 2 * mine.shape[2]
    vmem = pl.BlockSpec(memory_space=pltpu.VMEM)
    return pl.pallas_call(
        functools.partial(solve_kernel, cells_total, owned),
        in_specs=[vmem, vmem, vmem, vmem, vmem, pl.BlockSpec(memory_space=pltpu.SMEM)],
        out_specs=[vmem, vmem, vmem],
        out_shape=[
            jax.ShapeDtypeStruct((rank, owned), F32),
            jax.ShapeDtypeStruct(adjoint.shape, F32),
            jax.ShapeDtypeStruct(adjoint.shape, F32),
        ],
        scratch_shapes=[
            pltpu.VMEM((rank, 2 * rank), F32),
            pltpu.VMEM((rank, sketch), F32),
            pltpu.VMEM((rank, rank), F32),
            pltpu.VMEM((rank, rank), F32),
        ],
        compiler_params=pltpu.CompilerParams(vmem_limit_bytes=16 * 2**20),
        name="solve",
    )(crit, mine, range_t, adjoint, species, rates)


def partners(count, shift, other):
    return [(i, i ^ (other << shift)) for i in range(count)]


def member(shift, size):
    return (lax.axis_index(AXES) >> shift) & (size - 1)


def pick(pieces, index):
    return lax.dynamic_index_in_dim(pieces, index, 0, keepdims=False)


def summed_pieces(pieces, count, shift):
    size = pieces.shape[0]
    me = member(shift, size)
    got = [lax.ppermute(pick(pieces, me ^ p), AXES, partners(count, shift, p)) for p in ([2, 3, 1] if size == 4 and shift > 1 else range(size - 1, 0, -1))]
    total = pick(pieces, me)
    for piece in got:
        total = total + piece
    return total


def gathered_pieces(piece, count, shift, size):
    me = member(shift, size)
    got = [lax.ppermute(piece, AXES, partners(count, shift, p)) for p in range(size - 1, 0, -1)]
    out = jnp.zeros((size,) + piece.shape, piece.dtype)
    for p, part in zip([0] + list(range(size - 1, 0, -1)), [piece] + got):
        out = lax.dynamic_update_index_in_dim(out, part, me ^ p, 0)
    return out


def stages(count):
    bits = count.bit_length() - 1
    out, shift = [(0, 2)], 1
    while shift < bits:
        width = min(2, bits - shift)
        out.append((shift, 1 << width))
        shift += width
    return out


def reduce_sketches(crit, ct, range_t, count):
    plan = stages(count)
    halves, times, width = ct.shape
    owned = times // count
    left = count
    for shift, size in plan[:-1]:
        left //= size
        crit = crit.reshape(size, -1, width)
        ct = ct.reshape(halves, left, size, owned, width)
        ct = jnp.moveaxis(ct, 2, 0).reshape(size, -1, width)
        split = crit.shape[1]
        both = summed_pieces(jnp.concatenate([crit, ct], axis=1), count, shift)
        crit, ct = both[:split], both[split:].reshape(halves, left * owned, width)
    shift, size = plan[-1]
    crit, ct, range_t = lax.optimization_barrier((crit, ct, range_t))
    range_t = fetch(range_t)
    ct = ct.reshape(halves, size, owned, width)
    ct = jnp.moveaxis(ct, 1, 0).reshape(size, -1, width)
    split = crit.shape[0]
    whole = jnp.broadcast_to(crit[None], (size,) + crit.shape)
    both = summed_pieces(jnp.concatenate([whole, ct], axis=1), count, shift)
    crit, mine = both[:split], both[split:].reshape(halves, owned, width)
    for shift, size in plan[-2::-1]:
        crit = gathered_pieces(crit, count, shift, size).reshape(-1, width)
    return crit, mine, range_t


def shards(snapshots, range_test, test_rows, species, reaction_rates, adjoint_end):
    count = lax.axis_size(AXES)
    cells_total = snapshots.shape[0] * count
    range_t, ct, crit = sketches(snapshots, range_test, test_rows)
    crit, mine, range_t = reduce_sketches(crit, ct, range_t, count)
    time_factors, partial, rate = solve(crit, mine, range_t, adjoint_end, species, reaction_rates, cells_total)
    device = lax.axis_index(AXES)
    even = device % 2 == 0
    head = jnp.concatenate([partial[:1], adjoint_end[:1]], axis=0)
    tail = jnp.concatenate([partial[-1:], adjoint_end[-1:]], axis=0)
    pairs = [(i, i ^ 1) for i in range(count)]
    across = [(i, i + 1) for i in range(1, count - 1, 2)] + [(i + 1, i) for i in range(1, count - 1, 2)]
    near = lax.ppermute(jnp.where(even, tail, head), AXES, pairs)
    far = lax.ppermute(jnp.where(even, head, tail), AXES, across)
    above = jnp.where(even, far, near)
    below = jnp.where(even, near, far)
    adjoint = jnp.concatenate(
        [partial[:1] + DIFFUSION * above[1:], partial[1:-1], partial[-1:] + DIFFUSION * below[1:]], axis=0
    )
    top = jnp.where(device > 0, above[:1] + DIFFUSION * adjoint_end[:1], 0.0)
    bottom = jnp.where(device < count - 1, below[:1] + DIFFUSION * adjoint_end[-1:], 0.0)
    padded = jnp.concatenate([top, adjoint, bottom], axis=0)
    sideways = jnp.pad(adjoint, ((0, 0), (1, 1)))
    laplace = padded[2:] + padded[:-2] + sideways[:, 2:] + sideways[:, :-2] - 4.0 * adjoint
    return (adjoint + DIFFUSION * laplace + rate * adjoint, time_factors)


def solution(mesh):
    return jax.shard_map(
        shards,
        mesh=mesh,
        in_specs=(P(AXES, None), P(), P(None, AXES), P(AXES, None), P(), P(AXES, None)),
        out_specs=(P(AXES, None), P(None, AXES)),
        check_vma=False,
    )
```
